1024 devices in a mesh: dp: 2 (over core), expert: 64 (over z, y), tensor: 8 (over x).
Axes of the slice: x: 8, y: 8, z: 8, core: 2. Of those that a mesh axis runs over, the one named last changes fastest.
Arguments:
- tokens: bfloat16 [4096, 8192], P(('dp', 'expert')), may hold values from -6 to 6
- w_latent: bfloat16 [8192, 2048], P(None, 'tensor'), may hold values from -0.0625 to 0.0625
- w_gate: bfloat16 [64, 2048, 2048], P('expert', None, 'tensor'), may hold values from -0.125 to 0.125
- w_up: bfloat16 [64, 2048, 2048], P('expert', None, 'tensor'), may hold values from -0.125 to 0.125
- w_out: bfloat16 [64, 2048, 2048], P('expert', 'tensor'), may hold values from -0.125 to 0.125
- expert_ids: int32 [4096, 8], P(('dp', 'expert')), may hold values from 0 to 63, all different within a row; in each aligned block of 32 rows (0 to 31, 32 to 63, ...) at most 6 rows name the same one
- gates: bfloat16 [4096, 8], P(('dp', 'expert')), may hold values from 0.049804688 to 1
- cotangent: bfloat16 [4096, 2048], P(('dp', 'expert'), 'tensor'), may hold values from -6 to 6
Outputs:
- latent_out: bfloat16 [4096, 2048], P(('dp', 'expert'), 'tensor')
- latent_grad: bfloat16 [4096, 2048], P(('dp', 'expert'), 'tensor')
- grad_gate: bfloat16 [64, 2048, 2048], P('expert', 'dp', 'tensor')
- grad_up: bfloat16 [64, 2048, 2048], P('expert', 'dp', 'tensor')
- grad_out: bfloat16 [64, 2048, 2048], P('expert', 'tensor', 'dp')
The draws below stay inside these ranges and needn't reach their ends.
Inputs may be any that keep to these rules, and one draw needn't show every extreme that they name: `expert_ids`: each row names 8 different experts. In each aligned block of 32 rows (the rows of one data group) no expert is named by more than 6 rows, and in some blocks one expert is named by exactly 6.
All inputs are finite; a program needn't handle non-finite values.
Results may differ from the reference program's by a relative error of at most 0.0095.
Values may be sent and summed in bfloat16 or wider, within the bound.
A program may use at most 64 MiB of HBM per device.

```python
import math
import jax
import jax.numpy as jnp
import numpy as np
from jax import lax

D = 8192
L = 2048
H = 2048
TOP = 8
TOK_DEV = 32
EXPERTS = 64
CAP = 6
TOKENS = 4096
N_DP = 2
N_EXPERT = 64


def steps_of(rng, dims, shards, low, largest):
    level, own = 1.0, jax.random.fold_in(rng, 6)
    for axis_at, parts in shards:
        draws = jnp.exp(jax.random.uniform(jax.random.fold_in(own, axis_at), (parts,), jnp.float32, low / len(shards), largest / len(shards)))
        level = level * jnp.repeat(draws, dims[axis_at] // parts).reshape([-1 if axis == axis_at else 1 for axis in range(len(dims))])
    return level


def assign_block(own_key, own, number, rows, amount, top, most, skew):
    order = jax.random.permutation(own_key, amount)
    packed, common = portions_of(amount, rows * top, most, skew, True), portions_of(amount, rows * top, most, skew, False)
    places = jnp.arange(amount)

    def named(tallies, turn):
        used = int((tallies > 0).sum())
        fixed = max(1, used // 4)
        passed = fixed + (places - fixed + turn * (used - fixed)) % max(1, amount - fixed)
        return jnp.zeros((amount,), jnp.int32).at[order[jnp.where(places < fixed, places, passed)]].set(jnp.asarray(tallies, jnp.int32))

    tallies = jnp.where(number % 4 == 0, named(packed, number // 4), named(common, number - number // 4 - 1))
    mixed = jax.random.permutation(jax.random.fold_in(own, 3), amount)
    source_of, taker = mixed[0:amount // 2 * 2:2], mixed[1:amount // 2 * 2:2]
    margin = jnp.minimum(tallies[source_of] - 1, most - tallies[taker]) // 2
    margin = jnp.where((source_of == order[0]) | (taker == order[0]) | (tallies[taker] == 0), 0, jnp.maximum(margin, 0))
    passed = jax.random.randint(jax.random.fold_in(own, 4), (amount // 2,), 0, 1 << 20) % (margin + 1)
    tallies = tallies.at[source_of].add(-passed).at[taker].add(passed)
    members = jnp.searchsorted(jnp.cumsum(tallies), jnp.arange(rows * top), side="right").astype(jnp.int32)
    grid = members.reshape(top, rows).T
    grid = grid[jax.random.permutation(jax.random.fold_in(own, 1), rows)]
    turn = jax.random.randint(jax.random.fold_in(own, 2), (rows, 1), 0, top)
    return jnp.take_along_axis(grid, (jnp.arange(top)[None, :] + turn) % top, axis=1)


def portions_of(count, total, limit, skew, full):
    portions = [(1 << 20) // math.isqrt(standing ** skew) + 1 for standing in range(1, count + 1)]
    largest = limit if full else min(limit, max(-(-total // count), total * portions[0] // sum(portions)))
    least = 1 if total - largest >= count - 1 else 0
    given, rest = [largest] + [least] * (count - 1), total - largest - least * (count - 1)
    while rest > 0:
        candidates = [i for i in range(1, count) if given[i] < largest] or [i for i in range(1, count) if given[i] < limit]
        pool, remaining = sum([portions[i] for i in candidates]), rest
        for i in candidates:
            addition = min(limit - given[i], max(1, remaining * portions[i] // pool), rest)
            given[i] = given[i] + addition
            rest = rest - addition
    return np.array(given)


def normal_values(key, extent, spread, reach, pieces=(), held_as=jnp.bfloat16):
    array = spread * jax.random.normal(key, extent, jnp.float32)
    if pieces:
        array = array * steps_of(key, extent, pieces, -0.22, 0.18)
    return jnp.clip(array, -reach, reach).astype(held_as)


def setup_inputs(seed: int = 0) -> dict:
    key_list = jax.random.split(jax.random.key(seed), 9)
    tokens = normal_values(key_list[0], (TOKENS, D), 1.0, 6.0, ((0, 128),))
    w_latent = normal_values(key_list[1], (D, L), D ** -0.5, 0.0625, ((1, 8),))
    w_gate = normal_values(key_list[2], (EXPERTS, L, H), L ** -0.5, 0.125, ((0, 64), (2, 8)))
    w_up = normal_values(key_list[3], (EXPERTS, L, H), L ** -0.5, 0.125, ((0, 64), (2, 8)))
    w_out = normal_values(key_list[4], (EXPERTS, H, L), H ** -0.5, 0.125, ((0, 64), (1, 8)))
    expert_ids_keys = jax.random.split(jax.random.fold_in(key_list[5], 1), TOKENS // TOK_DEV)
    expert_ids_turns = jax.random.permutation(jax.random.fold_in(key_list[5], 3), TOKENS // TOK_DEV)
    expert_ids = jax.vmap(lambda own, number: assign_block(jax.random.fold_in(key_list[5], 2), own, number, TOK_DEV, EXPERTS, TOP, CAP, 2))(expert_ids_keys, expert_ids_turns).reshape((TOKENS, TOP))
    gates = jnp.clip(jnp.exp(math.log(1.0) - 2.9996462 * jax.random.uniform(key_list[6], (TOKENS, TOP), jnp.float32) ** steps_of(key_list[6], (TOKENS, TOP), ((0, 128),), -0.2, 0.2)), 0.049804688, 1.0).astype(jnp.bfloat16)
    cotangent = normal_values(key_list[7], (TOKENS, L), 1.0, 6.0, ((0, 128), (1, 8)))
    return {"tokens": tokens, "w_latent": w_latent, "w_gate": w_gate, "w_up": w_up, "w_out": w_out, "expert_ids": expert_ids, "gates": gates, "cotangent": cotangent}


def expert_pass(rows, cot_rows, weight_col, gate_matrix, up_matrix, out_matrix):
    pre_gate = jnp.dot(rows, gate_matrix, preferred_element_type=jnp.float32)
    pre_up = jnp.dot(rows, up_matrix, preferred_element_type=jnp.float32)
    gate_sigmoid = jax.nn.sigmoid(pre_gate)
    gate_silu = pre_gate * gate_sigmoid
    activated = (gate_silu * pre_up).astype(jnp.bfloat16)
    produced = (weight_col * jnp.dot(activated, out_matrix, preferred_element_type=jnp.float32)).astype(jnp.bfloat16)
    out_grad = (weight_col * cot_rows.astype(jnp.float32)).astype(jnp.bfloat16)
    act_grad = jnp.dot(out_grad, out_matrix.T, preferred_element_type=jnp.float32)
    gate_grad = (act_grad * pre_up * gate_sigmoid * (1.0 + pre_gate * (1.0 - gate_sigmoid))).astype(jnp.bfloat16)
    up_grad = (act_grad * gate_silu).astype(jnp.bfloat16)
    returned = (jnp.dot(gate_grad, gate_matrix.T, preferred_element_type=jnp.float32)
                + jnp.dot(up_grad, up_matrix.T, preferred_element_type=jnp.float32)).astype(jnp.bfloat16)
    grad_gate = jnp.dot(rows.T, gate_grad, preferred_element_type=jnp.float32).astype(jnp.bfloat16)
    grad_up = jnp.dot(rows.T, up_grad, preferred_element_type=jnp.float32).astype(jnp.bfloat16)
    grad_out = jnp.dot(activated.T, out_grad, preferred_element_type=jnp.float32).astype(jnp.bfloat16)
    return produced, returned, grad_gate, grad_up, grad_out


def reference(tokens, w_latent, w_gate, w_up, w_out, expert_ids, gates, cotangent):
    latent = jnp.dot(tokens, w_latent, preferred_element_type=jnp.float32).astype(jnp.bfloat16)
    flat_ids = expert_ids.reshape(-1).astype(jnp.int32)
    pair_total = flat_ids.shape[0]
    sorted_pairs = jnp.argsort(flat_ids, stable=True).astype(jnp.int32)
    counts = jnp.sum((flat_ids[:, None] == jnp.arange(EXPERTS, dtype=jnp.int32)[None, :]).astype(jnp.int32), axis=0)
    starts = (jnp.cumsum(counts) - counts).astype(jnp.int32)
    window = N_DP * N_EXPERT * CAP
    padded_order = jnp.concatenate([sorted_pairs, jnp.zeros((window,), jnp.int32)])
    flat_gates = gates.reshape(-1)
    lane_index = jnp.arange(window, dtype=jnp.int32)

    def take_window(first):
        return lax.dynamic_slice_in_dim(padded_order, first.astype(jnp.int32), window)

    def one_expert(expert):
        picked = take_window(starts[expert])
        live_mask = (lane_index < counts[expert]).astype(jnp.float32)
        token_rows = (picked // TOP).astype(jnp.int32)
        weight_col = (flat_gates[picked].astype(jnp.float32) * live_mask)[:, None]
        return expert_pass(latent[token_rows], cotangent[token_rows], weight_col,
                           w_gate[expert], w_up[expert], w_out[expert])

    produced, returned, grad_gate, grad_up, grad_out = lax.map(one_expert, jnp.arange(EXPERTS, dtype=jnp.int32))
    picked_all = jax.vmap(take_window)(starts).reshape(-1)
    out_pairs = jnp.zeros((pair_total, L), jnp.float32).at[picked_all].add(produced.reshape(-1, L).astype(jnp.float32))
    back_pairs = jnp.zeros((pair_total, L), jnp.float32).at[picked_all].add(returned.reshape(-1, L).astype(jnp.float32))
    latent_out = jnp.sum(out_pairs.reshape(-1, TOP, L), axis=1).astype(jnp.bfloat16)
    latent_grad = jnp.sum(back_pairs.reshape(-1, TOP, L), axis=1).astype(jnp.bfloat16)
    return latent_out, latent_grad, grad_gate, grad_up, grad_out
```

```python
import functools

import jax
import jax.numpy as jnp
from jax import lax
from jax.experimental import pallas as pl
from jax.experimental.pallas import tpu as pltpu
from jax.sharding import PartitionSpec as P

F32 = jnp.float32
BF16 = jnp.bfloat16
MESH = pl.DeviceIdType.MESH
CAP = 6
PAD = 8
R, L_ = 0, 1
OUT, BACK = 0, 1


def dot(a, b, contract):
    return lax.dot_general(a, b, (contract, ((), ())), preferred_element_type=F32)


NN = ((1,), (0,))
NT = ((1,), (1,))
TN = ((0,), (0,))


def slot_maps(ids, gates, groups):
    tok, top = ids.shape
    lane = lax.broadcasted_iota(jnp.int32, (tok, groups), 1)
    member = jnp.zeros((tok, groups), F32)
    weight = jnp.zeros((tok, groups), F32)
    for k in range(top):
        hit = ids[:, k : k + 1] == lane
        member = member + jnp.where(hit, 1.0, 0.0)
        weight = weight + jnp.where(hit, gates[:, k : k + 1].astype(F32), 0.0)
    earlier = lax.broadcasted_iota(jnp.int32, (tok, tok), 0) > lax.broadcasted_iota(
        jnp.int32, (tok, tok), 1
    )
    place = dot(jnp.where(earlier, 1.0, 0.0).astype(BF16), member.astype(BF16), NN)
    cols = groups * 2 * PAD
    widen = jnp.where(
        lax.shift_right_logical(lax.broadcasted_iota(jnp.int32, (groups, cols), 1), 4)
        == lax.broadcasted_iota(jnp.int32, (groups, cols), 0),
        1.0,
        0.0,
    ).astype(BF16)
    col = lax.broadcasted_iota(jnp.int32, (tok, cols), 1)
    slot = lax.bitwise_and(col, PAD - 1).astype(F32)
    part = lax.bitwise_and(col, PAD)
    here = jnp.where(
        dot(place.astype(BF16), widen, NN) == slot, dot(member.astype(BF16), widen, NN), 0.0
    )
    scaled = here * dot(weight.astype(BF16), widen, NN)
    return here, scaled, part == 0


def kernel(
    sizes,
    tokens,
    w_latent,
    w_gate,
    w_up,
    w_out,
    ids,
    gates,
    cot,
    latent_out,
    latent_grad,
    grad_gate,
    grad_up,
    grad_out,
    tok_v,
    wl_v,
    wgu,
    wo,
    comb,
    disp,
    land,
    ag,
    acc_h,
    acc_a,
    act,
    act_t,
    gug,
    rs_send,
    rs_recv,
    fin,
    ret,
    home,
    dp_gu_send,
    dp_gu_recv,
    dp_o_send,
    dp_o_recv,
    stage_gu,
    stage_o,
    load_sem,
    lat_sem,
    own_sem,
    a2a_send,
    a2a_recv,
    ag_send,
    ag_recv,
    rs_ssem,
    rs_rsem,
    dp_ssem,
    dp_rsem,
    store_sem,
):
    groups, ring, lat_steps, batch = sizes
    half = ring // 2
    wide = cot.shape[1]
    hid = wo.shape[1]
    rows = groups * CAP
    batches = groups // batch
    brow = batch * CAP
    tok = cot.shape[0]
    me_d, me_e, me_x = lax.axis_index("dp"), lax.axis_index("expert"), lax.axis_index("tensor")
    peer_d = 1 - me_d
    toward = (lax.rem(me_x + 1, ring), lax.rem(me_x + ring - 1, ring))

    barrier = pltpu.get_barrier_semaphore()

    @pl.loop(1, groups)
    def _(i):
        pl.semaphore_signal(
            barrier, 1, device_id={"expert": lax.rem(me_e + i, groups)}, device_id_type=MESH
        )

    for there in toward:
        pl.semaphore_signal(barrier, 1, device_id={"tensor": there}, device_id_type=MESH)
    pl.semaphore_signal(barrier, 1, device_id={"dp": peer_d}, device_id_type=MESH)

    depth = wl_v.shape[1]
    lat_copies = []
    for i in range(lat_steps):
        lat_copies.append(
            (
                pltpu.make_async_copy(
                    tokens.at[:, pl.ds(i * depth, depth)], tok_v.at[i], lat_sem.at[0, i]
                ),
                pltpu.make_async_copy(
                    w_latent.at[pl.ds(i * depth, depth), :], wl_v.at[i], lat_sem.at[1, i]
                ),
            )
        )
    for pair in lat_copies:
        for copy in pair:
            copy.start()
    weight_copies = []
    for i in range(ring):
        for which, copy_of in enumerate(
            (
                (w_gate.at[0, pl.ds(i * wide, wide), :], wgu.at[i, :, pl.ds(0, hid)]),
                (w_up.at[0, pl.ds(i * wide, wide), :], wgu.at[i, :, pl.ds(hid, hid)]),
                (w_out.at[0, :, pl.ds(i * wide, wide)], wo.at[i]),
            )
        ):
            copy = pltpu.make_async_copy(*copy_of, load_sem.at[which, i])
            copy.start()
            weight_copies.append(copy)

    here, scaled, forward = slot_maps(ids[...], gates[...], groups)
    comb[0] = jnp.where(forward, scaled, 0.0).astype(BF16)
    comb[1] = jnp.where(forward, 0.0, here).astype(BF16)
    to_rows = jnp.where(forward, here, 0.0).astype(BF16)
    to_cot = jnp.where(forward, 0.0, scaled).astype(BF16)
    latent = jnp.zeros((tok, wide), F32)
    for i, pair in enumerate(lat_copies):
        for copy in pair:
            copy.wait()
        latent = latent + dot(tok_v[i], wl_v[i], NN)
    disp[...] = (
        (dot(to_rows, latent.astype(BF16), TN) + dot(to_cot, cot[...], TN))
        .astype(BF16)
        .reshape(disp.shape)
    )
    pl.semaphore_wait(barrier, groups + 2)

    def exchange(src, dst, which):
        @pl.loop(1, groups)
        def _(i):
            there = lax.rem(me_e + i, groups)
            pltpu.make_async_remote_copy(
                src_ref=src.at[there],
                dst_ref=dst.at[me_e],
                send_sem=a2a_send.at[which],
                recv_sem=a2a_recv.at[which],
                device_id={"expert": there},
                device_id_type=MESH,
            ).start()

        own = pltpu.make_async_copy(src.at[me_e], dst.at[me_e], own_sem.at[which])
        own.start()
        own.wait()
        some = pl.ds(0, groups - 1)
        return pltpu.make_async_remote_copy(
            src_ref=src.at[some],
            dst_ref=dst.at[some],
            send_sem=a2a_send.at[which],
            recv_sem=a2a_recv.at[which],
            device_id={"expert": lax.rem(me_e + 1, groups)},
            device_id_type=MESH,
        )

    dispatch = exchange(disp, land, 0)

    def picks(shape, row_dim):
        col = lax.broadcasted_iota(jnp.int32, shape, 1 - row_dim)
        row = lax.broadcasted_iota(jnp.int32, shape, row_dim)
        slot = lax.bitwise_and(col, PAD - 1)
        part = lax.bitwise_and(lax.shift_right_logical(col, 3), 1)
        want = part * brow + lax.shift_right_logical(col, 4) * CAP + slot
        return jnp.where((row == want) & (slot < CAP), 1.0, 0.0).astype(BF16)

    block = batch * 2 * PAD
    squeeze = picks((2 * brow, block), 0)
    dispatch.wait_recv()
    for b in range(batches):
        packed = dot(squeeze, land[b * batch : (b + 1) * batch].reshape(block, wide), NN)
        packed = packed.astype(BF16)
        ag[me_x, OUT, pl.ds(b * brow, brow), :] = packed[:brow]
        ag[me_x, BACK, pl.ds(b * brow, brow), :] = packed[brow:]

    def ag_copy(way, part, step):
        back = step - 1
        owner = lax.rem(me_x + (ring - back if way == R else back), ring)
        return pltpu.make_async_remote_copy(
            src_ref=ag.at[owner, part],
            dst_ref=ag.at[owner, part],
            send_sem=ag_send.at[way, part, back],
            recv_sem=ag_recv.at[way, part, back],
            device_id={"tensor": toward[way]},
            device_id_type=MESH,
        )

    streams = ((R, OUT), (L_, BACK), (R, BACK), (L_, OUT))

    def last_of(way, part):
        return half if (way == R) == (part == OUT) else half - 1

    ag_copies = {
        (way, part, step): ag_copy(way, part, step)
        for way, part in streams
        for step in range(1, last_of(way, part) + 1)
    }
    for way, part in streams:
        if last_of(way, part) >= 1:
            ag_copies[way, part, 1].start()

    for copy in weight_copies:
        copy.wait()

    def absorb(owner, first=False):
        h = dot(ag[owner, OUT], wgu[owner], NN)
        a = dot(ag[owner, BACK], wo[owner], NT)
        if first:
            acc_h[...] = h
            acc_a[...] = a
        else:
            acc_h[...] += h
            acc_a[...] += a

    absorb(me_x, first=True)
    for step in range(1, half + 1):
        for way, part in streams:
            if step <= last_of(way, part):
                ag_copies[way, part, step].wait_recv()
                if step < last_of(way, part):
                    ag_copies[way, part, step + 1].start()
        absorb(lax.rem(me_x + ring - step, ring))
        if step < half:
            absorb(lax.rem(me_x + step, ring))

    pre_gate, pre_up, act_grad = acc_h[:, :hid], acc_h[:, hid:], acc_a[...]
    sig = jax.nn.sigmoid(pre_gate)
    silu = pre_gate * sig
    activated = silu * pre_up
    act[...] = activated.astype(BF16)
    gug[:, :hid] = (act_grad * pre_up * sig * (1.0 + pre_gate * (1.0 - sig))).astype(BF16)
    gug[:, hid:] = (act_grad * silu).astype(BF16)

    def contribution(part, owner):
        if part == OUT:
            return dot(act[...], wo[owner], NN)
        return dot(gug[...], wgu[owner], NT)

    def rs_copy(way, part, step):
        return pltpu.make_async_remote_copy(
            src_ref=rs_send.at[way, part, step - 1],
            dst_ref=rs_recv.at[way, part, step - 1],
            send_sem=rs_ssem.at[way, part, step - 1],
            recv_sem=rs_rsem.at[way, part, step - 1],
            device_id={"tensor": toward[way]},
            device_id_type=MESH,
        )

    rs_copies = {}

    def push(way, part, step):
        ahead = half + 1 - step
        owner = lax.rem(me_x + (ahead if way == R else ring - ahead), ring)
        value = contribution(part, owner)
        if (way, part, step - 1) in rs_copies:
            rs_copies[way, part, step - 1].wait_recv()
            value = value + rs_recv[way, part, step - 2].astype(F32)
        rs_send[way, part, step - 1] = value.astype(BF16)
        rs_copies[way, part, step] = rs_copy(way, part, step)
        rs_copies[way, part, step].start()

    push(R, OUT, 1)
    push(L_, BACK, 1)
    if half > 1:
        push(R, BACK, 2)
        push(L_, OUT, 2)

    act_t[...] = act[...].T
    dp_copies = []

    def grads_of(owner):
        return dot(ag[owner, OUT], gug[...], TN), dot(act_t[...], ag[owner, BACK], NN)

    def for_peer(i):
        gu, o = grads_of(peer_d * half + i)
        dp_gu_send[i] = gu.astype(BF16)
        dp_o_send[i] = o.astype(BF16)
        for j, (src, dst) in enumerate(((dp_gu_send, dp_gu_recv), (dp_o_send, dp_o_recv))):
            copy = pltpu.make_async_remote_copy(
                src_ref=src.at[i],
                dst_ref=dst.at[i],
                send_sem=dp_ssem.at[j, i],
                recv_sem=dp_rsem.at[j, i],
                device_id={"dp": peer_d},
                device_id_type=MESH,
            )
            copy.start()
            dp_copies.append(copy)

    stores = []

    def for_self(i):
        gu, o = grads_of(me_d * half + i)
        for copy in dp_copies[2 * i : 2 * i + 2]:
            copy.wait_recv()
        stage_gu[i] = (gu + dp_gu_recv[i].astype(F32)).astype(BF16)
        stage_o[i] = (o + dp_o_recv[i].astype(F32)).astype(BF16)
        for j, (src, dst) in enumerate(
            (
                (stage_gu.at[i, :, pl.ds(0, hid)], grad_gate.at[0, pl.ds(i * wide, wide), :]),
                (stage_gu.at[i, :, pl.ds(hid, hid)], grad_up.at[0, pl.ds(i * wide, wide), :]),
                (stage_o.at[i], grad_out.at[0, :, pl.ds(i * wide, wide)]),
            )
        ):
            copy = pltpu.make_async_copy(src, dst, store_sem.at[j, i])
            copy.start()
            stores.append(copy)

    tasks = [functools.partial(for_peer, i) for i in range(half)]
    tasks += [functools.partial(for_self, i) for i in range(half)]
    per_step = -(-len(tasks) // max(1, half - 1))
    for step in range(2, half + 1):
        for task in tasks[:per_step]:
            task()
        tasks = tasks[per_step:]
        push(R, OUT, step)
        push(L_, BACK, step)
        if step < half:
            push(R, BACK, step + 1)
            push(L_, OUT, step + 1)
    for task in tasks:
        task()

    for part in (OUT, BACK):
        total = contribution(part, me_x)
        for way in (R, L_):
            if (way, part, half) in rs_copies:
                rs_copies[way, part, half].wait_recv()
                total = total + rs_recv[way, part, half - 1].astype(F32)
        total = total.astype(BF16)
        for b in range(batches):
            fin[b, pl.ds(part * brow, brow), :] = total[b * brow : (b + 1) * brow]

    stretch = picks((block, 2 * brow), 1)
    for b in range(batches):
        spread = dot(stretch, fin[b], NN).astype(BF16)
        ret[b * batch : (b + 1) * batch] = spread.reshape(batch, 2 * PAD, wide)

    homeward = exchange(ret, home, 1)

    for copy in ag_copies.values():
        copy.wait_send()
    for copy in rs_copies.values():
        copy.wait_send()
    for copy in dp_copies:
        copy.wait_send()
    for copy in stores:
        copy.wait()
    dispatch.wait_send()

    homeward.wait_recv()
    back = home[...].reshape(groups * 2 * PAD, wide)
    latent_out[...] = dot(comb[0], back, NN).astype(BF16)
    latent_grad[...] = dot(comb[1], back, NN).astype(BF16)
    homeward.wait_send()


def per_device(tokens, w_latent, w_gate, w_up, w_out, expert_ids, gates, cotangent):
    groups, ring = lax.axis_size("expert"), lax.axis_size("tensor")
    half = ring // 2
    tok, width = tokens.shape
    wide = cotangent.shape[1]
    hid = w_gate.shape[2]
    rows = groups * CAP
    batch = min(16, groups)
    lat_steps = 8
    depth = width // lat_steps
    dma = pltpu.SemaphoreType.DMA
    vmem = pl.BlockSpec(memory_space=pltpu.VMEM)
    hbm = pl.BlockSpec(memory_space=pl.ANY)
    flops = 2 * tok * width * wide + 18 * rows * ring * wide * hid
    return pl.pallas_call(
        functools.partial(kernel, (groups, ring, lat_steps, batch)),
        out_shape=(
            jax.ShapeDtypeStruct((tok, wide), BF16),
            jax.ShapeDtypeStruct((tok, wide), BF16),
            jax.ShapeDtypeStruct((1, half * wide, hid), BF16),
            jax.ShapeDtypeStruct((1, half * wide, hid), BF16),
            jax.ShapeDtypeStruct((1, hid, half * wide), BF16),
        ),
        in_specs=[hbm] * 5 + [vmem] * 3,
        out_specs=(vmem, vmem, hbm, hbm, hbm),
        scratch_shapes=[
            pltpu.VMEM((lat_steps, tok, depth), BF16),
            pltpu.VMEM((lat_steps, depth, wide), BF16),
            pltpu.VMEM((ring, wide, 2 * hid), BF16),
            pltpu.VMEM((ring, hid, wide), BF16),
            pltpu.VMEM((2, tok, groups * 2 * PAD), BF16),
            pltpu.VMEM((groups, 2 * PAD, wide), BF16),
            pltpu.VMEM((groups, 2 * PAD, wide), BF16),
            pltpu.VMEM((ring, 2, rows, wide), BF16),
            pltpu.VMEM((rows, 2 * hid), F32),
            pltpu.VMEM((rows, hid), F32),
            pltpu.VMEM((rows, hid), BF16),
            pltpu.VMEM((hid, rows), BF16),
            pltpu.VMEM((rows, 2 * hid), BF16),
            pltpu.VMEM((2, 2, half, rows, wide), BF16),
            pltpu.VMEM((2, 2, half, rows, wide), BF16),
            pltpu.VMEM((groups // batch, 2 * batch * CAP, wide), BF16),
            pltpu.VMEM((groups, 2 * PAD, wide), BF16),
            pltpu.VMEM((groups, 2 * PAD, wide), BF16),
            pltpu.VMEM((half, wide, 2 * hid), BF16),
            pltpu.VMEM((half, wide, 2 * hid), BF16),
            pltpu.VMEM((half, hid, wide), BF16),
            pltpu.VMEM((half, hid, wide), BF16),
            pltpu.VMEM((half, wide, 2 * hid), BF16),
            pltpu.VMEM((half, hid, wide), BF16),
            dma((3, ring)),
            dma((2, lat_steps)),
            dma((2,)),
            dma((2,)),
            dma((2,)),
            dma((2, 2, half)),
            dma((2, 2, half)),
            dma((2, 2, half)),
            dma((2, 2, half)),
            dma((2, half)),
            dma((2, half)),
            dma((3, half)),
        ],
        compiler_params=pltpu.CompilerParams(
            collective_id=0, has_side_effects=True, vmem_limit_bytes=56 * 1024 * 1024
        ),
        cost_estimate=pl.CostEstimate(
            flops=flops, bytes_accessed=10 * 1024 * 1024, transcendentals=rows * hid
        ),
    )(tokens, w_latent, w_gate, w_up, w_out, expert_ids, gates, cotangent)


def solution(mesh):
    in_specs = (
        P(("dp", "expert"), None),
        P(None, "tensor"),
        P("expert", None, "tensor"),
        P("expert", None, "tensor"),
        P("expert", "tensor", None),
        P(("dp", "expert"), None),
        P(("dp", "expert"), None),
        P(("dp", "expert"), "tensor"),
    )
    out_specs = (
        P(("dp", "expert"), "tensor"),
        P(("dp", "expert"), "tensor"),
        P("expert", "dp", "tensor"),
        P("expert", "dp", "tensor"),
        P("expert", "tensor", "dp"),
    )
    return jax.shard_map(
        per_device, mesh=mesh, in_specs=in_specs, out_specs=out_specs, check_vma=False
    )
```

```python
import functools

import jax
import jax.numpy as jnp
from jax import lax
from jax.experimental import pallas as pl
from jax.experimental.pallas import tpu as pltpu
from jax.sharding import PartitionSpec as P

F32 = jnp.float32
BF16 = jnp.bfloat16
MESH = pl.DeviceIdType.MESH
CAP = 6
PAD = 8
R, L_ = 0, 1
OUT, BACK = 0, 1


def dot(a, b, contract):
    return lax.dot_general(a, b, (contract, ((), ())), preferred_element_type=F32)


NN = ((1,), (0,))
NT = ((1,), (1,))
TN = ((0,), (0,))


def slot_maps(ids, gates, groups):
    top, tok = ids.shape
    expert = lax.broadcasted_iota(jnp.int32, (groups, tok), 0)
    member = jnp.zeros((groups, tok), F32)
    weight = jnp.zeros((groups, tok), F32)
    for k in range(top):
        hit = ids[k : k + 1, :] == expert
        member = member + jnp.where(hit, 1.0, 0.0)
        weight = weight + jnp.where(hit, gates[k : k + 1, :].astype(F32), 0.0)
    earlier = lax.broadcasted_iota(jnp.int32, (tok, tok), 0) < lax.broadcasted_iota(
        jnp.int32, (tok, tok), 1
    )
    place = dot(member.astype(BF16), jnp.where(earlier, 1.0, 0.0).astype(BF16), NN)
    cols = groups * 2 * PAD
    widen = jnp.where(
        lax.shift_right_logical(lax.broadcasted_iota(jnp.int32, (groups, cols), 1), 4)
        == lax.broadcasted_iota(jnp.int32, (groups, cols), 0),
        1.0,
        0.0,
    ).astype(BF16)
    col = lax.broadcasted_iota(jnp.int32, (tok, cols), 1)
    slot = lax.bitwise_and(col, PAD - 1).astype(F32)
    part = lax.bitwise_and(col, PAD)
    here = jnp.where(
        dot(place.astype(BF16), widen, TN) == slot, dot(member.astype(BF16), widen, TN), 0.0
    )
    scaled = here * dot(weight.astype(BF16), widen, TN)
    return here, scaled, part == 0


def picks(shape, row_dim, brow):
    col = lax.broadcasted_iota(jnp.int32, shape, 1 - row_dim)
    row = lax.broadcasted_iota(jnp.int32, shape, row_dim)
    slot = lax.bitwise_and(col, PAD - 1)
    part = lax.bitwise_and(lax.shift_right_logical(col, 3), 1)
    want = part * brow + lax.shift_right_logical(col, 4) * CAP + slot
    return jnp.where((row == want) & (slot < CAP), 1.0, 0.0).astype(BF16)


def kernel(
    sizes,
    tokens,
    w_latent,
    w_gate,
    w_up,
    w_out,
    ids,
    gates,
    cot,
    latent_out,
    latent_grad,
    grad_gate,
    grad_up,
    grad_out,
    tok_v,
    wl_v,
    wgu,
    wo,
    comb,
    disp,
    land,
    ag,
    acc_h,
    acc_a,
    act,
    act_t,
    gug,
    rs_send,
    rs_recv,
    fin,
    ret,
    home,
    squeeze,
    stretch,
    dp_gu_send,
    dp_gu_recv,
    dp_o_send,
    dp_o_recv,
    stage_gu,
    stage_o,
    load_sem,
    lat_sem,
    own_sem,
    a2a_send,
    land_sem,
    home_sem,
    ag_send,
    ag_recv,
    rs_ssem,
    rs_rsem,
    dp_ssem,
    dp_rsem,
    store_sem,
):
    groups, span, ring, lat_steps = sizes
    lines = groups // span
    half = ring // 2
    wide = cot.shape[1]
    hid = wo.shape[1]
    batch, batches = 2 * span, lines // 2
    brow = batch * CAP
    rows = groups * CAP
    tok = cot.shape[0]
    block = batch * 2 * PAD
    me_d, me_e, me_x = lax.axis_index("dp"), lax.axis_index("expert"), lax.axis_index("tensor")
    peer_d = 1 - me_d
    toward = ((me_x + 1) % ring, (me_x + ring - 1) % ring)

    barrier = pltpu.get_barrier_semaphore()

    @pl.loop(1, groups)
    def _(i):
        pl.semaphore_signal(
            barrier, 1, device_id={"expert": (me_e + i) % groups}, device_id_type=MESH
        )

    for there in toward:
        pl.semaphore_signal(barrier, 1, device_id={"tensor": there}, device_id_type=MESH)
    pl.semaphore_signal(barrier, 1, device_id={"dp": peer_d}, device_id_type=MESH)

    depth = wl_v.shape[1]
    lat_copies = []
    for i in range(lat_steps):
        lat_copies.append(
            (
                pltpu.make_async_copy(
                    tokens.at[:, pl.ds(i * depth, depth)], tok_v.at[i], lat_sem.at[0, i]
                ),
                pltpu.make_async_copy(
                    w_latent.at[pl.ds(i * depth, depth), :], wl_v.at[i], lat_sem.at[1, i]
                ),
            )
        )
    for pair in lat_copies:
        for copy in pair:
            copy.start()
    weight_copies = []
    for i in range(ring):
        for which, copy_of in enumerate(
            (
                (w_gate.at[0, pl.ds(i * wide, wide), :], wgu.at[i, :, pl.ds(0, hid)]),
                (w_up.at[0, pl.ds(i * wide, wide), :], wgu.at[i, :, pl.ds(hid, hid)]),
                (w_out.at[0, :, pl.ds(i * wide, wide)], wo.at[i]),
            )
        ):
            copy = pltpu.make_async_copy(*copy_of, load_sem.at[which, i])
            copy.start()
            weight_copies.append(copy)

    here, scaled, forward = slot_maps(ids[...], gates[...], groups)
    comb[0] = jnp.where(forward, scaled, 0.0).astype(BF16)
    comb[1] = jnp.where(forward, 0.0, here).astype(BF16)
    to_rows = jnp.where(forward, here, 0.0).astype(BF16)
    to_cot = jnp.where(forward, 0.0, scaled).astype(BF16)
    latent = jnp.zeros((tok, wide), F32)
    for i, pair in enumerate(lat_copies):
        for copy in pair:
            copy.wait()
        latent = latent + dot(tok_v[i], wl_v[i], NN)
    disp[...] = (
        (dot(to_rows, latent.astype(BF16), TN) + dot(to_cot, cot[...], TN))
        .astype(BF16)
        .reshape(disp.shape)
    )
    squeeze[...] = picks((2 * brow, block), 0, brow)
    stretch[...] = picks((block, 2 * brow), 1, brow)
    pl.semaphore_wait(barrier, groups + 2)

    me_line, me_place = me_e // span, me_e % span

    def other(p, q, sign):
        odd, line_odd = (q // 2) % 2, q % 2
        by = q // 4
        d_place = by + odd * (span - 1 - 2 * by)
        d_line = p + line_odd * (lines - 1 - 2 * p)
        if sign < 0:
            d_place, d_line = span - d_place, lines - d_line
        return ((me_line + d_line) % lines) * span + (me_place + d_place) % span

    def dispatch_copy(p, q):
        there = other(p, q, 1)
        return pltpu.make_async_remote_copy(
            src_ref=disp.at[there],
            dst_ref=land.at[p * batch + q],
            send_sem=a2a_send.at[0],
            recv_sem=land_sem.at[p],
            device_id={"expert": there},
            device_id_type=MESH,
        )

    own = pltpu.make_async_copy(disp.at[me_e], land.at[0], own_sem.at[0])
    own.start()
    for p in range(batches):

        @pl.loop(1 if p == 0 else 0, batch)
        def _(q, p=p):
            dispatch_copy(p, q).start()

    def many(buffer, first, count, send_sem, recv_sem):
        part = buffer.at[pl.ds(first, count)]
        return pltpu.make_async_remote_copy(
            src_ref=part,
            dst_ref=part,
            send_sem=send_sem,
            recv_sem=recv_sem,
            device_id={"expert": (me_e + 1) % groups},
            device_id_type=MESH,
        )

    def passed(buffer, index, sems, way, p, step):
        send, recv = sems
        return pltpu.make_async_remote_copy(
            src_ref=buffer[0].at[index],
            dst_ref=buffer[1].at[index],
            send_sem=send.at[way, p, step - 1],
            recv_sem=recv.at[way, p, step - 1],
            device_id={"tensor": toward[way]},
            device_id_type=MESH,
        )

    halves = ((R, OUT), (L_, BACK))
    ag_copies, rs_copies, ret_copies, dp_copies, stores = {}, {}, [], [], []

    def gather(p, step):
        for way, part in halves:
            owner = (me_x + (ring - step + 1 if way == R else step - 1)) % ring
            index = (p, owner, part) if step == half else (p, owner)
            copy = passed((ag, ag), index, (ag_send, ag_recv), way, p, step)
            copy.start()
            ag_copies[way, p, step] = copy

    def absorb(p, owner, first=False):
        h = dot(ag[p, owner, OUT], wgu[owner], NN)
        a = dot(ag[p, owner, BACK], wo[owner], NT)
        if first:
            acc_h[p] = h
            acc_a[p] = a
        else:
            acc_h[p] += h
            acc_a[p] += a

    def enter(p):
        if p == 0:
            own.wait()
            many(land, 1, batch - 1, a2a_send.at[0], land_sem.at[0]).wait_recv()
        else:
            many(land, 0, batch, a2a_send.at[0], land_sem.at[p]).wait_recv()
        packed = dot(squeeze[...], land[p * batch : (p + 1) * batch].reshape(block, wide), NN)
        packed = packed.astype(BF16)
        ag[p, me_x, OUT] = packed[:brow]
        ag[p, me_x, BACK] = packed[brow:]
        gather(p, 1)
        if p == 0:
            for copy in weight_copies:
                copy.wait()
        absorb(p, me_x, first=True)

    def forward(p, step):
        for way in (R, L_):
            ag_copies[way, p, step].wait_recv()
        if step < half:
            gather(p, step + 1)
            absorb(p, (me_x + ring - step) % ring)
        absorb(p, (me_x + step) % ring)

    def activate(p):
        pre_gate, pre_up, act_grad = acc_h[p, :, :hid], acc_h[p, :, hid:], acc_a[p]
        sig = jax.nn.sigmoid(pre_gate)
        silu = pre_gate * sig
        act[p] = (silu * pre_up).astype(BF16)
        gug[p, :, :hid] = (act_grad * pre_up * sig * (1.0 + pre_gate * (1.0 - sig))).astype(BF16)
        gug[p, :, hid:] = (act_grad * silu).astype(BF16)

    def contribution(p, part, owner):
        if part == OUT:
            return dot(act[p], wo[owner], NN)
        return dot(gug[p], wgu[owner], NT)

    def push(p, step):
        ahead = half + 1 - step
        for way, part in halves:
            owner = (me_x + (ahead if way == R else ring - ahead)) % ring
            if step == 1:
                rs_send[way, p, 0, part] = contribution(p, part, owner).astype(BF16)
                index = (way, p, 0, part)
            else:
                values = [contribution(p, both, owner) for both in (OUT, BACK)]
                rs_copies[way, p, step - 1].wait_recv()
                for both in (OUT, BACK):
                    if step > 2 or both == part:
                        values[both] = values[both] + rs_recv[way, p, step - 2, both].astype(F32)
                    rs_send[way, p, step - 1, both] = values[both].astype(BF16)
                index = (way, p, step - 1)
            copy = passed((rs_send, rs_recv), index, (rs_ssem, rs_rsem), way, p, step)
            copy.start()
            rs_copies[way, p, step] = copy

    def leave(p):
        values = [contribution(p, both, me_x) for both in (OUT, BACK)]
        for way, part in halves:
            rs_copies[way, p, half].wait_recv()
            for both in (OUT, BACK):
                if half > 1 or both == part:
                    values[both] = values[both] + rs_recv[way, p, half - 1, both].astype(F32)
        for both in (OUT, BACK):
            fin[p, pl.ds(both * brow, brow), :] = values[both].astype(BF16)
        spread = dot(stretch[...], fin[p], NN).astype(BF16)
        ret[p * batch : (p + 1) * batch] = spread.reshape(batch, 2 * PAD, wide)

        @pl.loop(1 if p == 0 else 0, batch)
        def _(q):
            there = other(p, q, -1)
            pltpu.make_async_remote_copy(
                src_ref=ret.at[p * batch + q],
                dst_ref=home.at[me_e],
                send_sem=a2a_send.at[1],
                recv_sem=home_sem.at[0],
                device_id={"expert": there},
                device_id_type=MESH,
            ).start()

        if p == 0:
            ret_copies.append(pltpu.make_async_copy(ret.at[0], home.at[me_e], own_sem.at[1]))
            ret_copies[0].start()

    def grads_of(owner):
        lat = ag[:, owner, OUT].reshape(rows, wide)
        cots = ag[:, owner, BACK].reshape(rows, wide)
        return dot(lat, gug[...].reshape(rows, 2 * hid), TN), dot(act_t[...], cots, NN)

    def for_peer(i):
        if i == 0:
            act_t[...] = act[...].reshape(rows, hid).T
        gu, o = grads_of(peer_d * half + i)
        dp_gu_send[i] = gu.astype(BF16)
        dp_o_send[i] = o.astype(BF16)
        for j, (src, dst) in enumerate(((dp_gu_send, dp_gu_recv), (dp_o_send, dp_o_recv))):
            copy = pltpu.make_async_remote_copy(
                src_ref=src.at[i],
                dst_ref=dst.at[i],
                send_sem=dp_ssem.at[j, i],
                recv_sem=dp_rsem.at[j, i],
                device_id={"dp": peer_d},
                device_id_type=MESH,
            )
            copy.start()
            dp_copies.append(copy)

    def for_self(i):
        gu, o = grads_of(me_d * half + i)
        for copy in dp_copies[2 * i : 2 * i + 2]:
            copy.wait_recv()
        stage_gu[i] = (gu + dp_gu_recv[i].astype(F32)).astype(BF16)
        stage_o[i] = (o + dp_o_recv[i].astype(F32)).astype(BF16)
        for j, (src, dst) in enumerate(
            (
                (stage_gu.at[i, :, pl.ds(0, hid)], grad_gate.at[0, pl.ds(i * wide, wide), :]),
                (stage_gu.at[i, :, pl.ds(hid, hid)], grad_up.at[0, pl.ds(i * wide, wide), :]),
                (stage_o.at[i], grad_out.at[0, :, pl.ds(i * wide, wide)]),
            )
        ):
            copy = pltpu.make_async_copy(src, dst, store_sem.at[j, i])
            copy.start()
            stores.append(copy)

    tasks = [functools.partial(for_peer, i) for i in range(half)]
    tasks += [functools.partial(for_self, i) for i in range(half)]

    for tick in range(2 * half + batches):
        if tick < batches:
            enter(tick)
        for p in range(batches):
            at = tick - p
            if 1 <= at <= half:
                forward(p, at)
                if at == half:
                    activate(p)
                    push(p, 1)
            elif half < at < 2 * half:
                push(p, at - half + 1)
            elif at == 2 * half:
                leave(p)
            if tick > half + batches - 1 and tasks:
                tasks.pop(0)()
    for task in tasks:
        task()

    for copy in (*ag_copies.values(), *rs_copies.values(), *dp_copies):
        copy.wait_send()
    for copy in stores:
        copy.wait()
    many(disp, 0, groups - 1, a2a_send.at[0], land_sem.at[0]).wait_send()

    for copy in ret_copies:
        copy.wait()
    homeward = many(home, 0, groups - 1, a2a_send.at[1], home_sem.at[0])
    homeward.wait_recv()
    back = home[...].reshape(groups * 2 * PAD, wide)
    latent_out[...] = dot(comb[0], back, NN).astype(BF16)
    latent_grad[...] = dot(comb[1], back, NN).astype(BF16)
    homeward.wait_send()


def hand_on(*refs):
    count = (len(refs) - 1) // 2
    copies = [
        pltpu.make_async_copy(refs[i], refs[count + i], refs[-1].at[i]) for i in range(count)
    ]
    for copy in copies:
        copy.start()
    for copy in copies:
        copy.wait()


def per_device(tokens, w_latent, w_gate, w_up, w_out, expert_ids, gates, cotangent):
    groups, ring = lax.axis_size("expert"), lax.axis_size("tensor")
    half = ring // 2
    tok, width = tokens.shape
    wide = cotangent.shape[1]
    hid = w_gate.shape[2]
    rows = groups * CAP
    span = 1
    while (2 * span) ** 2 <= groups:
        span = 2 * span
    batch, batches = 2 * span, groups // (2 * span)
    brow, block = batch * CAP, batch * 2 * PAD
    lat_steps = 8
    depth = width // lat_steps
    dma = pltpu.SemaphoreType.DMA
    vmem = pl.BlockSpec(memory_space=pltpu.VMEM)
    hbm = pl.BlockSpec(memory_space=pl.ANY)
    flops = 2 * tok * width * wide + 18 * rows * ring * wide * hid
    outs = pl.pallas_call(
        functools.partial(kernel, (groups, span, ring, lat_steps)),
        out_shape=(
            jax.ShapeDtypeStruct((tok, wide), BF16),
            jax.ShapeDtypeStruct((tok, wide), BF16),
            jax.ShapeDtypeStruct((1, half * wide, hid), BF16),
            jax.ShapeDtypeStruct((1, half * wide, hid), BF16),
            jax.ShapeDtypeStruct((1, hid, half * wide), BF16),
        ),
        in_specs=[hbm] * 5 + [vmem] * 3,
        out_specs=(vmem, vmem, hbm, hbm, hbm),
        scratch_shapes=[
            pltpu.VMEM((lat_steps, tok, depth), BF16),
            pltpu.VMEM((lat_steps, depth, wide), BF16),
            pltpu.VMEM((ring, wide, 2 * hid), BF16),
            pltpu.VMEM((ring, hid, wide), BF16),
            pltpu.VMEM((2, tok, groups * 2 * PAD), BF16),
            pltpu.VMEM((groups, 2 * PAD, wide), BF16),
            pltpu.VMEM((groups, 2 * PAD, wide), BF16),
            pltpu.VMEM((batches, ring, 2, brow, wide), BF16),
            pltpu.VMEM((batches, brow, 2 * hid), F32),
            pltpu.VMEM((batches, brow, hid), F32),
            pltpu.VMEM((batches, brow, hid), BF16),
            pltpu.VMEM((hid, rows), BF16),
            pltpu.VMEM((batches, brow, 2 * hid), BF16),
            pltpu.VMEM((2, batches, half, 2, brow, wide), BF16),
            pltpu.VMEM((2, batches, half, 2, brow, wide), BF16),
            pltpu.VMEM((batches, 2 * brow, wide), BF16),
            pltpu.VMEM((groups, 2 * PAD, wide), BF16),
            pltpu.VMEM((groups, 2 * PAD, wide), BF16),
            pltpu.VMEM((2 * brow, block), BF16),
            pltpu.VMEM((block, 2 * brow), BF16),
            pltpu.VMEM((half, wide, 2 * hid), BF16),
            pltpu.VMEM((half, wide, 2 * hid), BF16),
            pltpu.VMEM((half, hid, wide), BF16),
            pltpu.VMEM((half, hid, wide), BF16),
            pltpu.VMEM((half, wide, 2 * hid), BF16),
            pltpu.VMEM((half, hid, wide), BF16),
            dma((3, ring)),
            dma((2, lat_steps)),
            dma((2,)),
            dma((2,)),
            dma((batches,)),
            dma((1,)),
            dma((2, batches, half)),
            dma((2, batches, half)),
            dma((2, batches, half)),
            dma((2, batches, half)),
            dma((2, half)),
            dma((2, half)),
            dma((3, half)),
        ],
        compiler_params=pltpu.CompilerParams(
            collective_id=0, has_side_effects=True, vmem_limit_bytes=56 * 1024 * 1024
        ),
        cost_estimate=pl.CostEstimate(
            flops=flops, bytes_accessed=10 * 1024 * 1024, transcendentals=rows * hid
        ),
    )(tokens, w_latent, w_gate, w_up, w_out, expert_ids.T, gates.T, cotangent)
    return pl.pallas_call(
        hand_on,
        out_shape=tuple(jax.ShapeDtypeStruct(out.shape, out.dtype) for out in outs),
        in_specs=[hbm] * len(outs),
        out_specs=(hbm,) * len(outs),
        scratch_shapes=[dma((len(outs),))],
    )(*outs)


def solution(mesh):
    in_specs = (
        P(("dp", "expert"), None),
        P(None, "tensor"),
        P("expert", None, "tensor"),
        P("expert", None, "tensor"),
        P("expert", "tensor", None),
        P(("dp", "expert"), None),
        P(("dp", "expert"), None),
        P(("dp", "expert"), "tensor"),
    )
    out_specs = (
        P(("dp", "expert"), "tensor"),
        P(("dp", "expert"), "tensor"),
        P("expert", "dp", "tensor"),
        P("expert", "dp", "tensor"),
        P("expert", "tensor", "dp"),
    )
    return jax.shard_map(
        per_device, mesh=mesh, in_specs=in_specs, out_specs=out_specs, check_vma=False
    )
```

```python
import functools

import jax
import jax.numpy as jnp
from jax import lax
from jax.experimental import pallas as pl
from jax.experimental.pallas import tpu as pltpu
from jax.sharding import PartitionSpec as P

F32 = jnp.float32
BF16 = jnp.bfloat16
MESH = pl.DeviceIdType.MESH
CAP = 6
PAD = 8
R, L_ = 0, 1
OUT, BACK = 0, 1


def dot(a, b, contract):
    return lax.dot_general(a, b, (contract, ((), ())), preferred_element_type=F32)


NN = ((1,), (0,))
NT = ((1,), (1,))
TN = ((0,), (0,))


def slot_maps(ids, gates, groups):
    top, tok = ids.shape
    expert = lax.broadcasted_iota(jnp.int32, (groups, tok), 0)
    member = jnp.zeros((groups, tok), F32)
    weight = jnp.zeros((groups, tok), F32)
    for k in range(top):
        hit = ids[k : k + 1, :] == expert
        member = member + jnp.where(hit, 1.0, 0.0)
        weight = weight + jnp.where(hit, gates[k : k + 1, :].astype(F32), 0.0)
    earlier = lax.broadcasted_iota(jnp.int32, (tok, tok), 0) < lax.broadcasted_iota(
        jnp.int32, (tok, tok), 1
    )
    place = dot(member.astype(BF16), jnp.where(earlier, 1.0, 0.0).astype(BF16), NN)
    cols = groups * 2 * PAD
    widen = jnp.where(
        lax.shift_right_logical(lax.broadcasted_iota(jnp.int32, (groups, cols), 1), 4)
        == lax.broadcasted_iota(jnp.int32, (groups, cols), 0),
        1.0,
        0.0,
    ).astype(BF16)
    col = lax.broadcasted_iota(jnp.int32, (tok, cols), 1)
    slot = lax.bitwise_and(col, PAD - 1).astype(F32)
    part = lax.bitwise_and(col, PAD)
    here = jnp.where(
        dot(place.astype(BF16), widen, TN) == slot, dot(member.astype(BF16), widen, TN), 0.0
    )
    scaled = here * dot(weight.astype(BF16), widen, TN)
    return here, scaled, part == 0


def picks(shape, row_dim, brow):
    col = lax.broadcasted_iota(jnp.int32, shape, 1 - row_dim)
    row = lax.broadcasted_iota(jnp.int32, shape, row_dim)
    slot = lax.bitwise_and(col, PAD - 1)
    part = lax.bitwise_and(lax.shift_right_logical(col, 3), 1)
    want = part * brow + lax.shift_right_logical(col, 4) * CAP + slot
    return jnp.where((row == want) & (slot < CAP), 1.0, 0.0).astype(BF16)


def kernel(
    sizes,
    tokens,
    w_latent,
    w_gate,
    w_up,
    w_out,
    ids,
    gates,
    cot,
    latent_out,
    latent_grad,
    grad_gate,
    grad_up,
    grad_out,
    tok_v,
    wl_v,
    wgu,
    wo,
    comb,
    disp,
    land,
    ag,
    acc_h,
    acc_a,
    act,
    act_t,
    gug,
    rs_send,
    rs_recv,
    fin,
    ret,
    home,
    squeeze,
    stretch,
    dp_gu_send,
    dp_gu_recv,
    dp_o_send,
    dp_o_recv,
    stage_gu,
    stage_o,
    load_sem,
    lat_sem,
    own_sem,
    a2a_send,
    land_sem,
    home_sem,
    ag_send,
    ag_recv,
    rs_ssem,
    rs_rsem,
    dp_ssem,
    dp_rsem,
    store_sem,
):
    groups, span, ring, lat_steps = sizes
    lines = groups // span
    half = ring // 2
    wide = cot.shape[1]
    hid = wo.shape[1]
    batch, batches = 2 * span, lines // 2
    brow = batch * CAP
    rows = groups * CAP
    tok = cot.shape[0]
    block = batch * 2 * PAD
    me_d, me_e, me_x = lax.axis_index("dp"), lax.axis_index("expert"), lax.axis_index("tensor")
    peer_d = 1 - me_d
    toward = ((me_x + 1) % ring, (me_x + ring - 1) % ring)

    barrier = pltpu.get_barrier_semaphore()

    @pl.loop(1, groups)
    def _(i):
        pl.semaphore_signal(
            barrier, 1, device_id={"expert": (me_e + i) % groups}, device_id_type=MESH
        )

    for there in toward:
        pl.semaphore_signal(barrier, 1, device_id={"tensor": there}, device_id_type=MESH)
    pl.semaphore_signal(barrier, 1, device_id={"dp": peer_d}, device_id_type=MESH)

    depth = wl_v.shape[1]
    lat_copies = []
    for i in range(lat_steps):
        lat_copies.append(
            (
                pltpu.make_async_copy(
                    tokens.at[:, pl.ds(i * depth, depth)], tok_v.at[i], lat_sem.at[0, i]
                ),
                pltpu.make_async_copy(
                    w_latent.at[pl.ds(i * depth, depth), :], wl_v.at[i], lat_sem.at[1, i]
                ),
            )
        )
    for pair in lat_copies:
        for copy in pair:
            copy.start()
    weight_copies = []
    for i in range(ring):
        for which, copy_of in enumerate(
            (
                (w_gate.at[0, pl.ds(i * wide, wide), :], wgu.at[i, :, pl.ds(0, hid)]),
                (w_up.at[0, pl.ds(i * wide, wide), :], wgu.at[i, :, pl.ds(hid, hid)]),
                (w_out.at[0, :, pl.ds(i * wide, wide)], wo.at[i]),
            )
        ):
            copy = pltpu.make_async_copy(*copy_of, load_sem.at[which, i])
            copy.start()
            weight_copies.append(copy)

    here, scaled, forward = slot_maps(ids[...], gates[...], groups)
    comb[0] = jnp.where(forward, scaled, 0.0).astype(BF16)
    comb[1] = jnp.where(forward, 0.0, here).astype(BF16)
    to_rows = jnp.where(forward, here, 0.0).astype(BF16)
    to_cot = jnp.where(forward, 0.0, scaled).astype(BF16)
    latent = jnp.zeros((tok, wide), F32)
    for i, pair in enumerate(lat_copies):
        for copy in pair:
            copy.wait()
        latent = latent + dot(tok_v[i], wl_v[i], NN)
    disp[...] = (
        (dot(to_rows, latent.astype(BF16), TN) + dot(to_cot, cot[...], TN))
        .astype(BF16)
        .reshape(disp.shape)
    )
    squeeze[...] = picks((2 * brow, block), 0, brow)
    stretch[...] = picks((block, 2 * brow), 1, brow)
    pl.semaphore_wait(barrier, groups + 2)

    me_line, me_place = me_e // span, me_e % span

    def other(p, q, sign):
        odd, line_odd = (q // 2) % 2, q % 2
        by = q // 4
        d_place = by + odd * (span - 1 - 2 * by)
        d_line = p + line_odd * (lines - 1 - 2 * p)
        if sign < 0:
            d_place, d_line = span - d_place, lines - d_line
        return ((me_line + d_line) % lines) * span + (me_place + d_place) % span

    def dispatch_copy(p, q):
        there = other(p, q, 1)
        return pltpu.make_async_remote_copy(
            src_ref=disp.at[there],
            dst_ref=land.at[p * batch + q],
            send_sem=a2a_send.at[0],
            recv_sem=land_sem.at[p],
            device_id={"expert": there},
            device_id_type=MESH,
        )

    own = pltpu.make_async_copy(disp.at[me_e], land.at[0], own_sem.at[0])
    own.start()
    for p in range(batches):

        @pl.loop(1 if p == 0 else 0, batch)
        def _(q, p=p):
            dispatch_copy(p, q).start()

    def many(buffer, first, count, send_sem, recv_sem):
        part = buffer.at[pl.ds(first, count)]
        return pltpu.make_async_remote_copy(
            src_ref=part,
            dst_ref=part,
            send_sem=send_sem,
            recv_sem=recv_sem,
            device_id={"expert": (me_e + 1) % groups},
            device_id_type=MESH,
        )

    def passed(buffer, index, sems, way, p, step):
        send, recv = sems
        return pltpu.make_async_remote_copy(
            src_ref=buffer[0].at[index],
            dst_ref=buffer[1].at[index],
            send_sem=send.at[way, p, step - 1],
            recv_sem=recv.at[way, p, step - 1],
            device_id={"tensor": toward[way]},
            device_id_type=MESH,
        )

    halves = ((R, OUT), (L_, BACK))
    ag_copies, rs_copies, ret_copies, dp_copies, stores = {}, {}, [], [], []

    def gather(p, step):
        for way, part in halves:
            owner = (me_x + (ring - step + 1 if way == R else step - 1)) % ring
            index = (p, owner, part) if step == half else (p, owner)
            copy = passed((ag, ag), index, (ag_send, ag_recv), way, p, step)
            copy.start()
            ag_copies[way, p, step] = copy

    def absorb(p, owner, first=False):
        h = dot(ag[p, owner, OUT], wgu[owner], NN)
        a = dot(ag[p, owner, BACK], wo[owner], NT)
        if first:
            acc_h[p] = h
            acc_a[p] = a
        else:
            acc_h[p] += h
            acc_a[p] += a

    def enter(p):
        if p == 0:
            own.wait()
            many(land, 1, batch - 1, a2a_send.at[0], land_sem.at[0]).wait_recv()
        else:
            many(land, 0, batch, a2a_send.at[0], land_sem.at[p]).wait_recv()
        packed = dot(squeeze[...], land[p * batch : (p + 1) * batch].reshape(block, wide), NN)
        packed = packed.astype(BF16)
        ag[p, me_x, OUT] = packed[:brow]
        ag[p, me_x, BACK] = packed[brow:]
        gather(p, 1)
        if p == 0:
            for copy in weight_copies:
                copy.wait()
        absorb(p, me_x, first=True)

    def forward(p, step):
        for way in (R, L_):
            ag_copies[way, p, step].wait_recv()
        if step < half:
            gather(p, step + 1)
            absorb(p, (me_x + ring - step) % ring)
        absorb(p, (me_x + step) % ring)

    def activate(p):
        pre_gate, pre_up, act_grad = acc_h[p, :, :hid], acc_h[p, :, hid:], acc_a[p]
        sig = jax.nn.sigmoid(pre_gate)
        silu = pre_gate * sig
        act[p] = (silu * pre_up).astype(BF16)
        gug[p, :, :hid] = (act_grad * pre_up * sig * (1.0 + pre_gate * (1.0 - sig))).astype(BF16)
        gug[p, :, hid:] = (act_grad * silu).astype(BF16)

    def contribution(p, part, owner):
        if part == OUT:
            return dot(act[p], wo[owner], NN)
        return dot(gug[p], wgu[owner], NT)

    def push(p, step):
        ahead = half + 1 - step
        for way, part in halves:
            owner = (me_x + (ahead if way == R else ring - ahead)) % ring
            if step == 1:
                rs_send[way, p, 0, part] = contribution(p, part, owner).astype(BF16)
                index = (way, p, 0, part)
            else:
                values = [contribution(p, both, owner) for both in (OUT, BACK)]
                rs_copies[way, p, step - 1].wait_recv()
                for both in (OUT, BACK):
                    if step > 2 or both == part:
                        values[both] = values[both] + rs_recv[way, p, step - 2, both].astype(F32)
                    rs_send[way, p, step - 1, both] = values[both].astype(BF16)
                index = (way, p, step - 1)
            copy = passed((rs_send, rs_recv), index, (rs_ssem, rs_rsem), way, p, step)
            copy.start()
            rs_copies[way, p, step] = copy

    def leave(p):
        values = [contribution(p, both, me_x) for both in (OUT, BACK)]
        for way, part in halves:
            rs_copies[way, p, half].wait_recv()
            for both in (OUT, BACK):
                if half > 1 or both == part:
                    values[both] = values[both] + rs_recv[way, p, half - 1, both].astype(F32)
        for both in (OUT, BACK):
            fin[p, pl.ds(both * brow, brow), :] = values[both].astype(BF16)
        spread = dot(stretch[...], fin[p], NN).astype(BF16)
        ret[p * batch : (p + 1) * batch] = spread.reshape(batch, 2 * PAD, wide)

        @pl.loop(1 if p == 0 else 0, batch)
        def _(q):
            there = other(p, q, -1)
            pltpu.make_async_remote_copy(
                src_ref=ret.at[p * batch + q],
                dst_ref=home.at[me_e],
                send_sem=a2a_send.at[1],
                recv_sem=home_sem.at[0],
                device_id={"expert": there},
                device_id_type=MESH,
            ).start()

        if p == 0:
            ret_copies.append(pltpu.make_async_copy(ret.at[0], home.at[me_e], own_sem.at[1]))
            ret_copies[0].start()

    def grads_of(owner):
        lat = ag[:, owner, OUT].reshape(rows, wide)
        cots = ag[:, owner, BACK].reshape(rows, wide)
        return dot(lat, gug[...].reshape(rows, 2 * hid), TN), dot(act_t[...], cots, NN)

    def for_peer(i):
        if i == 0:
            act_t[...] = act[...].reshape(rows, hid).T
        gu, o = grads_of(peer_d * half + i)
        dp_gu_send[i] = gu.astype(BF16)
        dp_o_send[i] = o.astype(BF16)
        for j, (src, dst) in enumerate(((dp_gu_send, dp_gu_recv), (dp_o_send, dp_o_recv))):
            copy = pltpu.make_async_remote_copy(
                src_ref=src.at[i],
                dst_ref=dst.at[i],
                send_sem=dp_ssem.at[j, i],
                recv_sem=dp_rsem.at[j, i],
                device_id={"dp": peer_d},
                device_id_type=MESH,
            )
            copy.start()
            dp_copies.append(copy)

    def for_self(i):
        gu, o = grads_of(me_d * half + i)
        for copy in dp_copies[2 * i : 2 * i + 2]:
            copy.wait_recv()
        stage_gu[i] = (gu + dp_gu_recv[i].astype(F32)).astype(BF16)
        stage_o[i] = (o + dp_o_recv[i].astype(F32)).astype(BF16)
        for j, (src, dst) in enumerate(
            (
                (stage_gu.at[i, :, pl.ds(0, hid)], grad_gate.at[0, pl.ds(i * wide, wide), :]),
                (stage_gu.at[i, :, pl.ds(hid, hid)], grad_up.at[0, pl.ds(i * wide, wide), :]),
                (stage_o.at[i], grad_out.at[0, :, pl.ds(i * wide, wide)]),
            )
        ):
            copy = pltpu.make_async_copy(src, dst, store_sem.at[j, i])
            copy.start()
            stores.append(copy)

    tasks = [functools.partial(for_peer, i) for i in range(half)]
    tasks += [functools.partial(for_self, i) for i in range(half)]

    for tick in range(2 * half + batches):
        if tick < batches:
            enter(tick)
        for p in reversed(range(batches)):
            at = tick - p
            if 1 <= at <= half:
                forward(p, at)
                if at == half:
                    activate(p)
                    push(p, 1)
            elif half < at < 2 * half:
                push(p, at - half + 1)
            elif at == 2 * half:
                leave(p)
            if tick > half + batches - 1 and tasks:
                tasks.pop(0)()
    for task in tasks:
        task()

    for copy in (*ag_copies.values(), *rs_copies.values(), *dp_copies):
        copy.wait_send()
    for copy in stores:
        copy.wait()
    many(disp, 0, groups - 1, a2a_send.at[0], land_sem.at[0]).wait_send()

    for copy in ret_copies:
        copy.wait()
    homeward = many(home, 0, groups - 1, a2a_send.at[1], home_sem.at[0])
    homeward.wait_recv()
    back = home[...].reshape(groups * 2 * PAD, wide)
    latent_out[...] = dot(comb[0], back, NN).astype(BF16)
    latent_grad[...] = dot(comb[1], back, NN).astype(BF16)
    homeward.wait_send()


def hand_on(count, *refs):
    given, results, held = refs[:count], refs[count : 2 * count], refs[2 * count : 3 * count]
    sems = refs[-1]
    loads = [pltpu.make_async_copy(given[i], held[i], sems.at[0, i]) for i in range(count)]
    stores = [pltpu.make_async_copy(held[i], results[i], sems.at[1, i]) for i in range(count)]
    for copy in loads:
        copy.start()
    for load, store in zip(loads, stores):
        load.wait()
        store.start()
    for copy in stores:
        copy.wait()


def per_device(tokens, w_latent, w_gate, w_up, w_out, expert_ids, gates, cotangent):
    groups, ring = lax.axis_size("expert"), lax.axis_size("tensor")
    half = ring // 2
    tok, width = tokens.shape
    wide = cotangent.shape[1]
    hid = w_gate.shape[2]
    rows = groups * CAP
    span = 1
    while (2 * span) ** 2 <= groups:
        span = 2 * span
    batch, batches = 2 * span, groups // (2 * span)
    brow, block = batch * CAP, batch * 2 * PAD
    lat_steps = 8
    depth = width // lat_steps
    dma = pltpu.SemaphoreType.DMA
    vmem = pl.BlockSpec(memory_space=pltpu.VMEM)
    hbm = pl.BlockSpec(memory_space=pl.ANY)
    flops = 2 * tok * width * wide + 18 * rows * ring * wide * hid
    outs = pl.pallas_call(
        functools.partial(kernel, (groups, span, ring, lat_steps)),
        out_shape=(
            jax.ShapeDtypeStruct((tok, wide), BF16),
            jax.ShapeDtypeStruct((tok, wide), BF16),
            jax.ShapeDtypeStruct((1, half * wide, hid), BF16),
            jax.ShapeDtypeStruct((1, half * wide, hid), BF16),
            jax.ShapeDtypeStruct((1, hid, half * wide), BF16),
        ),
        in_specs=[hbm] * 5 + [vmem] * 3,
        out_specs=(vmem, vmem, hbm, hbm, hbm),
        scratch_shapes=[
            pltpu.VMEM((lat_steps, tok, depth), BF16),
            pltpu.VMEM((lat_steps, depth, wide), BF16),
            pltpu.VMEM((ring, wide, 2 * hid), BF16),
            pltpu.VMEM((ring, hid, wide), BF16),
            pltpu.VMEM((2, tok, groups * 2 * PAD), BF16),
            pltpu.VMEM((groups, 2 * PAD, wide), BF16),
            pltpu.VMEM((groups, 2 * PAD, wide), BF16),
            pltpu.VMEM((batches, ring, 2, brow, wide), BF16),
            pltpu.VMEM((batches, brow, 2 * hid), F32),
            pltpu.VMEM((batches, brow, hid), F32),
            pltpu.VMEM((batches, brow, hid), BF16),
            pltpu.VMEM((hid, rows), BF16),
            pltpu.VMEM((batches, brow, 2 * hid), BF16),
            pltpu.VMEM((2, batches, half, 2, brow, wide), BF16),
            pltpu.VMEM((2, batches, half, 2, brow, wide), BF16),
            pltpu.VMEM((batches, 2 * brow, wide), BF16),
            pltpu.VMEM((groups, 2 * PAD, wide), BF16),
            pltpu.VMEM((groups, 2 * PAD, wide), BF16),
            pltpu.VMEM((2 * brow, block), BF16),
            pltpu.VMEM((block, 2 * brow), BF16),
            pltpu.VMEM((half, wide, 2 * hid), BF16),
            pltpu.VMEM((half, wide, 2 * hid), BF16),
            pltpu.VMEM((half, hid, wide), BF16),
            pltpu.VMEM((half, hid, wide), BF16),
            pltpu.VMEM((half, wide, 2 * hid), BF16),
            pltpu.VMEM((half, hid, wide), BF16),
            dma((3, ring)),
            dma((2, lat_steps)),
            dma((2,)),
            dma((2,)),
            dma((batches,)),
            dma((1,)),
            dma((2, batches, half)),
            dma((2, batches, half)),
            dma((2, batches, half)),
            dma((2, batches, half)),
            dma((2, half)),
            dma((2, half)),
            dma((3, half)),
        ],
        compiler_params=pltpu.CompilerParams(
            collective_id=0, has_side_effects=True, vmem_limit_bytes=56 * 1024 * 1024
        ),
        cost_estimate=pl.CostEstimate(
            flops=flops, bytes_accessed=10 * 1024 * 1024, transcendentals=rows * hid
        ),
    )(tokens, w_latent, w_gate, w_up, w_out, expert_ids.T, gates.T, cotangent)
    return pl.pallas_call(
        functools.partial(hand_on, len(outs)),
        out_shape=tuple(jax.ShapeDtypeStruct(out.shape, out.dtype) for out in outs),
        in_specs=[hbm] * len(outs),
        out_specs=(hbm,) * len(outs),
        scratch_shapes=[pltpu.VMEM(out.shape, out.dtype) for out in outs] + [dma((2, len(outs)))],
        compiler_params=pltpu.CompilerParams(vmem_limit_bytes=60 * 1024 * 1024),
    )(*outs)


def solution(mesh):
    in_specs = (
        P(("dp", "expert"), None),
        P(None, "tensor"),
        P("expert", None, "tensor"),
        P("expert", None, "tensor"),
        P("expert", "tensor", None),
        P(("dp", "expert"), None),
        P(("dp", "expert"), None),
        P(("dp", "expert"), "tensor"),
    )
    out_specs = (
        P(("dp", "expert"), "tensor"),
        P(("dp", "expert"), "tensor"),
        P("expert", "dp", "tensor"),
        P("expert", "dp", "tensor"),
        P("expert", "tensor", "dp"),
    )
    return jax.shard_map(
        per_device, mesh=mesh, in_specs=in_specs, out_specs=out_specs, check_vma=False
    )
```

```python
import functools

import jax
import jax.numpy as jnp
from jax import lax
from jax.experimental import pallas as pl
from jax.experimental.pallas import tpu as pltpu
from jax.sharding import PartitionSpec as P

F32 = jnp.float32
BF16 = jnp.bfloat16
MESH = pl.DeviceIdType.MESH
CAP = 6
PAD = 8
R, L_ = 0, 1
OUT, BACK = 0, 1


def dot(a, b, contract):
    return lax.dot_general(a, b, (contract, ((), ())), preferred_element_type=F32)


NN = ((1,), (0,))
NT = ((1,), (1,))
TN = ((0,), (0,))


def slot_maps(ids, gates, groups):
    top, tok = ids.shape
    expert = lax.broadcasted_iota(jnp.int32, (groups, tok), 0)
    member = jnp.zeros((groups, tok), F32)
    weight = jnp.zeros((groups, tok), F32)
    for k in range(top):
        hit = ids[k : k + 1, :] == expert
        member = member + jnp.where(hit, 1.0, 0.0)
        weight = weight + jnp.where(hit, gates[k : k + 1, :].astype(F32), 0.0)
    earlier = lax.broadcasted_iota(jnp.int32, (tok, tok), 0) < lax.broadcasted_iota(
        jnp.int32, (tok, tok), 1
    )
    place = dot(member.astype(BF16), jnp.where(earlier, 1.0, 0.0).astype(BF16), NN)
    cols = groups * 2 * PAD
    widen = jnp.where(
        lax.shift_right_logical(lax.broadcasted_iota(jnp.int32, (groups, cols), 1), 4)
        == lax.broadcasted_iota(jnp.int32, (groups, cols), 0),
        1.0,
        0.0,
    ).astype(BF16)
    col = lax.broadcasted_iota(jnp.int32, (tok, cols), 1)
    slot = lax.bitwise_and(col, PAD - 1).astype(F32)
    part = lax.bitwise_and(col, PAD)
    here = jnp.where(
        dot(place.astype(BF16), widen, TN) == slot, dot(member.astype(BF16), widen, TN), 0.0
    )
    scaled = here * dot(weight.astype(BF16), widen, TN)
    return here, scaled, part == 0


def picks(shape, row_dim, brow):
    col = lax.broadcasted_iota(jnp.int32, shape, 1 - row_dim)
    row = lax.broadcasted_iota(jnp.int32, shape, row_dim)
    slot = lax.bitwise_and(col, PAD - 1)
    part = lax.bitwise_and(lax.shift_right_logical(col, 3), 1)
    want = part * brow + lax.shift_right_logical(col, 4) * CAP + slot
    return jnp.where((row == want) & (slot < CAP), 1.0, 0.0).astype(BF16)


def kernel(
    sizes,
    tokens,
    w_latent,
    w_gate,
    w_up,
    w_out,
    ids,
    gates,
    cot,
    latent_out,
    latent_grad,
    grad_gate,
    grad_up,
    grad_out,
    tok_v,
    wl_v,
    wgu,
    wo,
    comb,
    disp,
    land,
    ag,
    acc_h,
    acc_a,
    act,
    act_t,
    gug,
    rs_send,
    rs_recv,
    fin,
    ret,
    home,
    squeeze,
    stretch,
    dp_gu_send,
    dp_gu_recv,
    dp_o_send,
    dp_o_recv,
    stage_gu,
    stage_o,
    load_sem,
    lat_sem,
    own_sem,
    a2a_send,
    land_sem,
    home_sem,
    ag_send,
    ag_recv,
    rs_ssem,
    rs_rsem,
    dp_ssem,
    dp_rsem,
    store_sem,
):
    groups, span, ring, lat_steps = sizes
    lines = groups // span
    half = ring // 2
    wide = cot.shape[1]
    hid = wo.shape[1]
    batch, batches = 2 * span, lines // 2
    brow = batch * CAP
    rows = groups * CAP
    tok = cot.shape[0]
    block = batch * 2 * PAD
    me_d, me_e, me_x = lax.axis_index("dp"), lax.axis_index("expert"), lax.axis_index("tensor")
    peer_d = 1 - me_d
    toward = ((me_x + 1) % ring, (me_x + ring - 1) % ring)

    depth = wl_v.shape[1]
    lat_copies = []
    for i in range(lat_steps):
        lat_copies.append(
            (
                pltpu.make_async_copy(
                    tokens.at[:, pl.ds(i * depth, depth)], tok_v.at[i], lat_sem.at[0, i]
                ),
                pltpu.make_async_copy(
                    w_latent.at[pl.ds(i * depth, depth), :], wl_v.at[i], lat_sem.at[1, i]
                ),
            )
        )
    for pair in lat_copies:
        for copy in pair:
            copy.start()
    barrier = pltpu.get_barrier_semaphore()

    @pl.loop(1, groups)
    def _(i):
        pl.semaphore_signal(
            barrier, 1, device_id={"expert": (me_e + i) % groups}, device_id_type=MESH
        )

    for there in toward:
        pl.semaphore_signal(barrier, 1, device_id={"tensor": there}, device_id_type=MESH)
    pl.semaphore_signal(barrier, 1, device_id={"dp": peer_d}, device_id_type=MESH)

    weight_copies = [
        pltpu.make_async_copy(w_gate, wgu.at[:, :, pl.ds(0, hid)], load_sem.at[0]),
        pltpu.make_async_copy(w_up, wgu.at[:, :, pl.ds(hid, hid)], load_sem.at[1]),
    ]
    for i in range(ring):
        part = w_out.at[0, :, pl.ds(i * wide, wide)]
        weight_copies.append(pltpu.make_async_copy(part, wo.at[i], load_sem.at[2 + i]))
    for copy in weight_copies:
        copy.start()

    here, scaled, forward = slot_maps(ids[...], gates[...], groups)
    comb[0] = jnp.where(forward, scaled, 0.0).astype(BF16)
    comb[1] = jnp.where(forward, 0.0, here).astype(BF16)
    to_rows = jnp.where(forward, here, 0.0).astype(BF16)
    to_cot = jnp.where(forward, 0.0, scaled).astype(BF16)
    latent = jnp.zeros((tok, wide), F32)
    for i, pair in enumerate(lat_copies):
        for copy in pair:
            copy.wait()
        latent = latent + dot(tok_v[i], wl_v[i], NN)
    disp[...] = (
        (dot(to_rows, latent.astype(BF16), TN) + dot(to_cot, cot[...], TN))
        .astype(BF16)
        .reshape(disp.shape)
    )
    squeeze[...] = picks((2 * brow, block), 0, brow)
    stretch[...] = picks((block, 2 * brow), 1, brow)
    pl.semaphore_wait(barrier, groups + 2)

    me_line, me_place = me_e // span, me_e % span

    def to_batch(p, sign, send):
        lines_there = [
            (me_line + (by if sign > 0 else lines - by)) % lines for by in (p, lines - 1 - p)
        ]

        def four(by, skip):
            for odd in (0, 1):
                place = by + odd * (span - 1 - 2 * by)
                place_there = (me_place + (place if sign > 0 else span - place)) % span
                for line_odd in (0, 1):
                    if not (skip and odd == 0 and line_odd == 0):
                        q = 4 * by + 2 * odd + line_odd
                        send(p * batch + q, lines_there[line_odd] * span + place_there)

        if p == 0:
            four(0, True)
        if p > 0 or span > 2:
            pl.loop(1 if p == 0 else 0, span // 2)(lambda by: four(by, False))

    def dispatch(p):
        def send(index, there):
            pltpu.make_async_remote_copy(
                src_ref=disp.at[there],
                dst_ref=land.at[index],
                send_sem=a2a_send.at[0],
                recv_sem=land_sem.at[p],
                device_id={"expert": there},
                device_id_type=MESH,
            ).start()

        to_batch(p, 1, send)

    order = [*range(1, batches), 0]
    own = pltpu.make_async_copy(disp.at[me_e], land.at[0], own_sem.at[0])
    own.start()
    for p in order[:2]:
        dispatch(p)

    def many(buffer, first, count, send_sem, recv_sem):
        part = buffer.at[pl.ds(first, count)]
        return pltpu.make_async_remote_copy(
            src_ref=part,
            dst_ref=part,
            send_sem=send_sem,
            recv_sem=recv_sem,
            device_id={"expert": (me_e + 1) % groups},
            device_id_type=MESH,
        )

    def passed(buffer, index, sems, way, p, step):
        send, recv = sems
        return pltpu.make_async_remote_copy(
            src_ref=buffer[0].at[index],
            dst_ref=buffer[1].at[index],
            send_sem=send.at[way, p, step - 1],
            recv_sem=recv.at[way, p, step - 1],
            device_id={"tensor": toward[way]},
            device_id_type=MESH,
        )

    halves = ((R, OUT), (L_, BACK))
    ag_copies, rs_copies, ret_copies, dp_copies, stores = {}, {}, [], [], []

    def gather(p, step):
        for way, part in halves:
            owner = (me_x + (ring - step + 1 if way == R else step - 1)) % ring
            index = (p, owner, part) if step == half else (p, owner)
            copy = passed((ag, ag), index, (ag_send, ag_recv), way, p, step)
            copy.start()
            ag_copies[way, p, step] = copy

    def absorb(p, owner, first=False):
        h = dot(ag[p, owner, OUT], wgu[owner], NN)
        a = dot(ag[p, owner, BACK], wo[owner], NT)
        if first:
            acc_h[p] = h
            acc_a[p] = a
        else:
            acc_h[p] += h
            acc_a[p] += a

    def enter(p):
        if p == 0:
            own.wait()
            many(land, 1, batch - 1, a2a_send.at[0], land_sem.at[0]).wait_recv()
        else:
            many(land, 0, batch, a2a_send.at[0], land_sem.at[p]).wait_recv()
        packed = dot(squeeze[...], land[p * batch : (p + 1) * batch].reshape(block, wide), NN)
        packed = packed.astype(BF16)
        ag[p, me_x, OUT] = packed[:brow]
        ag[p, me_x, BACK] = packed[brow:]
        gather(p, 1)
        if p in order[:-2]:
            dispatch(order[order.index(p) + 2])
        if p == order[0]:
            for copy in weight_copies:
                copy.wait()
        absorb(p, me_x, first=True)

    def forward(p, step):
        for way in (R, L_):
            ag_copies[way, p, step].wait_recv()
        if step < half:
            gather(p, step + 1)
            absorb(p, (me_x + ring - step) % ring)
        absorb(p, (me_x + step) % ring)

    def activate(p):
        pre_gate, pre_up, act_grad = acc_h[p, :, :hid], acc_h[p, :, hid:], acc_a[p]
        sig = jax.nn.sigmoid(pre_gate)
        silu = pre_gate * sig
        act[p] = (silu * pre_up).astype(BF16)
        gug[p, :, :hid] = (act_grad * pre_up * sig * (1.0 + pre_gate * (1.0 - sig))).astype(BF16)
        gug[p, :, hid:] = (act_grad * silu).astype(BF16)

    def contribution(p, part, owner):
        if part == OUT:
            return dot(act[p], wo[owner], NN)
        return dot(gug[p], wgu[owner], NT)

    def push(p, step):
        ahead = half + 1 - step
        for way, part in halves:
            owner = (me_x + (ahead if way == R else ring - ahead)) % ring
            if step == 1:
                rs_send[way, p, 0, part] = contribution(p, part, owner).astype(BF16)
                index = (way, p, 0, part)
            else:
                values = [contribution(p, both, owner) for both in (OUT, BACK)]
                rs_copies[way, p, step - 1].wait_recv()
                for both in (OUT, BACK):
                    if step > 2 or both == part:
                        values[both] = values[both] + rs_recv[way, p, step - 2, both].astype(F32)
                    rs_send[way, p, step - 1, both] = values[both].astype(BF16)
                index = (way, p, step - 1)
            copy = passed((rs_send, rs_recv), index, (rs_ssem, rs_rsem), way, p, step)
            copy.start()
            rs_copies[way, p, step] = copy

    def leave(p):
        values = [contribution(p, both, me_x) for both in (OUT, BACK)]
        for way, part in halves:
            rs_copies[way, p, half].wait_recv()
            for both in (OUT, BACK):
                if half > 1 or both == part:
                    values[both] = values[both] + rs_recv[way, p, half - 1, both].astype(F32)
        for both in (OUT, BACK):
            fin[p, pl.ds(both * brow, brow), :] = values[both].astype(BF16)
        spread = dot(stretch[...], fin[p], NN).astype(BF16)
        ret[p * batch : (p + 1) * batch] = spread.reshape(batch, 2 * PAD, wide)

        def send(index, there):
            pltpu.make_async_remote_copy(
                src_ref=ret.at[index],
                dst_ref=home.at[me_e],
                send_sem=a2a_send.at[1],
                recv_sem=home_sem.at[0],
                device_id={"expert": there},
                device_id_type=MESH,
            ).start()

        to_batch(p, -1, send)

        if p == 0:
            ret_copies.append(pltpu.make_async_copy(ret.at[0], home.at[me_e], own_sem.at[1]))
            ret_copies[0].start()

    def grads_of(owner):
        lat = ag[:, owner, OUT].reshape(rows, wide)
        cots = ag[:, owner, BACK].reshape(rows, wide)
        return dot(lat, gug[...].reshape(rows, 2 * hid), TN), dot(act_t[...], cots, NN)

    def for_peer(i):
        if i == 0:
            act_t[...] = act[...].reshape(rows, hid).T
        gu, o = grads_of(peer_d * half + i)
        dp_gu_send[i] = gu.astype(BF16)
        dp_o_send[i] = o.astype(BF16)
        for j, (src, dst) in enumerate(((dp_gu_send, dp_gu_recv), (dp_o_send, dp_o_recv))):
            copy = pltpu.make_async_remote_copy(
                src_ref=src.at[i],
                dst_ref=dst.at[i],
                send_sem=dp_ssem.at[j, i],
                recv_sem=dp_rsem.at[j, i],
                device_id={"dp": peer_d},
                device_id_type=MESH,
            )
            copy.start()
            dp_copies.append(copy)

    def for_self(i):
        gu, o = grads_of(me_d * half + i)
        for copy in dp_copies[2 * i : 2 * i + 2]:
            copy.wait_recv()
        stage_gu[i] = (gu + dp_gu_recv[i].astype(F32)).astype(BF16)
        stage_o[i] = (o + dp_o_recv[i].astype(F32)).astype(BF16)
        for j, (src, dst) in enumerate(
            (
                (stage_gu.at[i, :, pl.ds(0, hid)], grad_gate.at[0, pl.ds(i * wide, wide), :]),
                (stage_gu.at[i, :, pl.ds(hid, hid)], grad_up.at[0, pl.ds(i * wide, wide), :]),
                (stage_o.at[i], grad_out.at[0, :, pl.ds(i * wide, wide)]),
            )
        ):
            copy = pltpu.make_async_copy(src, dst, store_sem.at[j, i])
            copy.start()
            stores.append(copy)

    tasks = [functools.partial(for_peer, i) for i in range(half)]
    tasks += [functools.partial(for_self, i) for i in range(half)]

    for tick in range(2 * half + batches):
        if tick < batches:
            enter(order[tick])
        for place, p in reversed(list(enumerate(order))):
            at = tick - place
            if 1 <= at <= half:
                forward(p, at)
                if at == half:
                    activate(p)
                    push(p, 1)
            elif half < at < 2 * half:
                push(p, at - half + 1)
            elif at == 2 * half:
                leave(p)
            if tick > half + batches - 1 and tasks:
                tasks.pop(0)()
    for task in tasks:
        task()

    for copy in (*ag_copies.values(), *rs_copies.values(), *dp_copies):
        copy.wait_send()
    for copy in stores:
        copy.wait()
    many(disp, 0, groups - 1, a2a_send.at[0], land_sem.at[0]).wait_send()

    for copy in ret_copies:
        copy.wait()
    homeward = many(home, 0, groups - 1, a2a_send.at[1], home_sem.at[0])
    homeward.wait_recv()
    back = home[...].reshape(groups * 2 * PAD, wide)
    latent_out[...] = dot(comb[0], back, NN).astype(BF16)
    latent_grad[...] = dot(comb[1], back, NN).astype(BF16)
    homeward.wait_send()


def hand_on(count, *refs):
    given, results, held = refs[:count], refs[count : 2 * count], refs[2 * count : 3 * count]
    sems = refs[-1]
    loads = [pltpu.make_async_copy(given[i], held[i], sems.at[0, i]) for i in range(count)]
    stores = [pltpu.make_async_copy(held[i], results[i], sems.at[1, i]) for i in range(count)]
    for copy in loads:
        copy.start()
    for load, store in zip(loads, stores):
        load.wait()
        store.start()
    for copy in stores:
        copy.wait()


def per_device(tokens, w_latent, w_gate, w_up, w_out, expert_ids, gates, cotangent):
    groups, ring = lax.axis_size("expert"), lax.axis_size("tensor")
    half = ring // 2
    tok, width = tokens.shape
    wide = cotangent.shape[1]
    hid = w_gate.shape[2]
    rows = groups * CAP
    span = 1
    while (2 * span) ** 2 <= groups:
        span = 2 * span
    batch, batches = 2 * span, groups // (2 * span)
    brow, block = batch * CAP, batch * 2 * PAD
    lat_steps = 8
    depth = width // lat_steps
    dma = pltpu.SemaphoreType.DMA
    vmem = pl.BlockSpec(memory_space=pltpu.VMEM)
    hbm = pl.BlockSpec(memory_space=pl.ANY)
    flops = 2 * tok * width * wide + 18 * rows * ring * wide * hid
    outs = pl.pallas_call(
        functools.partial(kernel, (groups, span, ring, lat_steps)),
        out_shape=(
            jax.ShapeDtypeStruct((tok, wide), BF16),
            jax.ShapeDtypeStruct((tok, wide), BF16),
            jax.ShapeDtypeStruct((1, half * wide, hid), BF16),
            jax.ShapeDtypeStruct((1, half * wide, hid), BF16),
            jax.ShapeDtypeStruct((1, hid, half * wide), BF16),
        ),
        in_specs=[hbm] * 5 + [vmem] * 3,
        out_specs=(vmem, vmem, hbm, hbm, hbm),
        scratch_shapes=[
            pltpu.VMEM((lat_steps, tok, depth), BF16),
            pltpu.VMEM((lat_steps, depth, wide), BF16),
            pltpu.VMEM((ring, wide, 2 * hid), BF16),
            pltpu.VMEM((ring, hid, wide), BF16),
            pltpu.VMEM((2, tok, groups * 2 * PAD), BF16),
            pltpu.VMEM((groups, 2 * PAD, wide), BF16),
            pltpu.VMEM((groups, 2 * PAD, wide), BF16),
            pltpu.VMEM((batches, ring, 2, brow, wide), BF16),
            pltpu.VMEM((batches, brow, 2 * hid), F32),
            pltpu.VMEM((batches, brow, hid), F32),
            pltpu.VMEM((batches, brow, hid), BF16),
            pltpu.VMEM((hid, rows), BF16),
            pltpu.VMEM((batches, brow, 2 * hid), BF16),
            pltpu.VMEM((2, batches, half, 2, brow, wide), BF16),
            pltpu.VMEM((2, batches, half, 2, brow, wide), BF16),
            pltpu.VMEM((batches, 2 * brow, wide), BF16),
            pltpu.VMEM((groups, 2 * PAD, wide), BF16),
            pltpu.VMEM((groups, 2 * PAD, wide), BF16),
            pltpu.VMEM((2 * brow, block), BF16),
            pltpu.VMEM((block, 2 * brow), BF16),
            pltpu.VMEM((half, wide, 2 * hid), BF16),
            pltpu.VMEM((half, wide, 2 * hid), BF16),
            pltpu.VMEM((half, hid, wide), BF16),
            pltpu.VMEM((half, hid, wide), BF16),
            pltpu.VMEM((half, wide, 2 * hid), BF16),
            pltpu.VMEM((half, hid, wide), BF16),
            dma((2 + ring,)),
            dma((2, lat_steps)),
            dma((2,)),
            dma((2,)),
            dma((batches,)),
            dma((1,)),
            dma((2, batches, half)),
            dma((2, batches, half)),
            dma((2, batches, half)),
            dma((2, batches, half)),
            dma((2, half)),
            dma((2, half)),
            dma((3, half)),
        ],
        compiler_params=pltpu.CompilerParams(
            collective_id=0, has_side_effects=True, vmem_limit_bytes=56 * 1024 * 1024
        ),
        cost_estimate=pl.CostEstimate(
            flops=flops, bytes_accessed=10 * 1024 * 1024, transcendentals=rows * hid
        ),
    )(
        tokens,
        w_latent,
        w_gate.reshape(ring, wide, hid),
        w_up.reshape(ring, wide, hid),
        w_out,
        expert_ids.T,
        gates.T,
        cotangent,
    )
    return pl.pallas_call(
        functools.partial(hand_on, len(outs)),
        out_shape=tuple(jax.ShapeDtypeStruct(out.shape, out.dtype) for out in outs),
        in_specs=[hbm] * len(outs),
        out_specs=(hbm,) * len(outs),
        scratch_shapes=[pltpu.VMEM(out.shape, out.dtype) for out in outs] + [dma((2, len(outs)))],
        compiler_params=pltpu.CompilerParams(vmem_limit_bytes=60 * 1024 * 1024),
    )(*outs)


def solution(mesh):
    in_specs = (
        P(("dp", "expert"), None),
        P(None, "tensor"),
        P("expert", None, "tensor"),
        P("expert", None, "tensor"),
        P("expert", "tensor", None),
        P(("dp", "expert"), None),
        P(("dp", "expert"), None),
        P(("dp", "expert"), "tensor"),
    )
    out_specs = (
        P(("dp", "expert"), "tensor"),
        P(("dp", "expert"), "tensor"),
        P("expert", "dp", "tensor"),
        P("expert", "dp", "tensor"),
        P("expert", "tensor", "dp"),
    )
    return jax.shard_map(
        per_device, mesh=mesh, in_specs=in_specs, out_specs=out_specs, check_vma=False
    )
```

```python
import functools

import jax
import jax.numpy as jnp
from jax import lax
from jax.experimental import pallas as pl
from jax.experimental.pallas import tpu as pltpu
from jax.sharding import PartitionSpec as P

F32 = jnp.float32
BF16 = jnp.bfloat16
MESH = pl.DeviceIdType.MESH
CAP = 6
PAD = 8
R, L_ = 0, 1
OUT, BACK = 0, 1


def dot(a, b, contract):
    return lax.dot_general(a, b, (contract, ((), ())), preferred_element_type=F32)


NN = ((1,), (0,))
NT = ((1,), (1,))
TN = ((0,), (0,))


def slot_maps(ids, gates, groups, near):
    top, tok = ids.shape
    expert = lax.broadcasted_iota(jnp.int32, (groups, tok), 0)
    member = jnp.zeros((groups, tok), F32)
    weight = jnp.zeros((groups, tok), F32)
    for k in range(top):
        hit = ids[k : k + 1, :] == expert
        member = member + jnp.where(hit, 1.0, 0.0)
        weight = weight + jnp.where(hit, gates[k : k + 1, :].astype(F32), 0.0)
    earlier = lax.broadcasted_iota(jnp.int32, (tok, tok), 0) < lax.broadcasted_iota(
        jnp.int32, (tok, tok), 1
    )
    place = dot(member.astype(BF16), jnp.where(earlier, 1.0, 0.0).astype(BF16), NN)

    def spread(cols, owner_of):
        widen = jnp.where(
            owner_of(lax.broadcasted_iota(jnp.int32, (groups, cols), 1))
            == lax.broadcasted_iota(jnp.int32, (groups, cols), 0),
            1.0,
            0.0,
        ).astype(BF16)
        col = lax.broadcasted_iota(jnp.int32, (tok, cols), 1)
        slot = lax.bitwise_and(col, PAD - 1).astype(F32)
        here = jnp.where(
            dot(place.astype(BF16), widen, TN) == slot, dot(member.astype(BF16), widen, TN), 0.0
        )
        return here, here * dot(weight.astype(BF16), widen, TN), lax.bitwise_and(col, PAD) == 0

    return (
        spread(groups * 2 * PAD, lambda col: lax.shift_right_logical(col, 4)),
        spread(near[0] * 2 * PAD, near[1]),
    )


def picks(shape, row_dim, brow):
    col = lax.broadcasted_iota(jnp.int32, shape, 1 - row_dim)
    row = lax.broadcasted_iota(jnp.int32, shape, row_dim)
    slot = lax.bitwise_and(col, PAD - 1)
    part = lax.bitwise_and(lax.shift_right_logical(col, 3), 1)
    want = part * brow + lax.shift_right_logical(col, 4) * CAP + slot
    return jnp.where((row == want) & (slot < CAP), 1.0, 0.0).astype(BF16)


def kernel(
    sizes,
    tokens,
    w_latent,
    w_gate,
    w_up,
    w_out,
    ids,
    gates,
    cot,
    latent_out,
    latent_grad,
    grad_gate,
    grad_up,
    grad_out,
    tok_v,
    wl_v,
    wgu,
    wo,
    comb,
    disp,
    land,
    ag,
    acc_h,
    acc_a,
    act,
    act_t,
    gug,
    rs_send,
    rs_recv,
    fin,
    ret,
    home,
    squeeze,
    stretch,
    near_map,
    cot_all,
    disp_wide,
    land_wide,
    dp_gu_send,
    dp_gu_recv,
    dp_o_send,
    dp_o_recv,
    stage_gu,
    stage_o,
    load_sem,
    lat_sem,
    own_sem,
    a2a_send,
    land_sem,
    home_sem,
    wide_sem,
    cot_send,
    cot_recv,
    ag_send,
    ag_recv,
    rs_ssem,
    rs_rsem,
    dp_ssem,
    dp_rsem,
    store_sem,
):
    groups, span, ring, lat_steps = sizes
    lines = groups // span
    half = ring // 2
    wide = cot.shape[1]
    hid = wo.shape[1]
    batch, batches = 2 * span, lines // 2
    brow = batch * CAP
    rows = groups * CAP
    tok = cot.shape[0]
    block = batch * 2 * PAD
    me_d, me_e, me_x = lax.axis_index("dp"), lax.axis_index("expert"), lax.axis_index("tensor")
    peer_d = 1 - me_d
    toward = ((me_x + 1) % ring, (me_x + ring - 1) % ring)

    depth = wl_v.shape[1]
    lat_copies = []
    for i in range(lat_steps):
        lat_copies.append(
            (
                pltpu.make_async_copy(
                    tokens.at[:, pl.ds(i * depth, depth)], tok_v.at[i], lat_sem.at[0, i]
                ),
                pltpu.make_async_copy(
                    w_latent.at[pl.ds(i * depth, depth), :], wl_v.at[i], lat_sem.at[1, i]
                ),
            )
        )
    for pair in lat_copies:
        for copy in pair:
            copy.start()
    barrier = pltpu.get_barrier_semaphore()

    @pl.loop(1, groups)
    def _(i):
        pl.semaphore_signal(
            barrier, 1, device_id={"expert": (me_e + i) % groups}, device_id_type=MESH
        )

    for i in range(1, ring):
        pl.semaphore_signal(
            barrier, 1, device_id={"tensor": (me_x + i) % ring}, device_id_type=MESH
        )
    pl.semaphore_signal(barrier, 1, device_id={"dp": peer_d}, device_id_type=MESH)

    weight_copies = [
        pltpu.make_async_copy(w_gate, wgu.at[:, :, pl.ds(0, hid)], load_sem.at[0]),
        pltpu.make_async_copy(w_up, wgu.at[:, :, pl.ds(hid, hid)], load_sem.at[1]),
    ]
    for i in range(ring):
        part = w_out.at[0, :, pl.ds(i * wide, wide)]
        weight_copies.append(pltpu.make_async_copy(part, wo.at[i], load_sem.at[2 + i]))
    for copy in weight_copies:
        copy.start()

    me_line, me_place = me_e // span, me_e % span

    def near_expert(col):
        q = lax.shift_right_logical(col, 4)
        by = lax.shift_right_logical(q, 2)
        odd = lax.bitwise_and(lax.shift_right_logical(q, 1), 1)
        place = by + odd * (span - 1 - 2 * by)
        line = lax.bitwise_and(q, 1) * (lines - 1)
        return lax.bitwise_and(me_line + line, lines - 1) * span + lax.bitwise_and(
            me_place + place, span - 1
        )

    maps = slot_maps(ids[...], gates[...], groups, (batch, near_expert))
    (here, scaled, forward), (_, near_scaled, near_first) = maps
    near_map[0] = jnp.where(near_first, near_scaled, 0.0).astype(BF16)
    near_map[1] = jnp.where(near_first, 0.0, near_scaled).astype(BF16)
    cot_all[me_x] = cot[...]
    comb[0] = jnp.where(forward, scaled, 0.0).astype(BF16)
    comb[1] = jnp.where(forward, 0.0, here).astype(BF16)
    to_rows = jnp.where(forward, here, 0.0).astype(BF16)
    to_cot = jnp.where(forward, 0.0, scaled).astype(BF16)
    latent = jnp.zeros((tok, wide), F32)
    for i, pair in enumerate(lat_copies):
        for copy in pair:
            copy.wait()
        latent = latent + dot(tok_v[i], wl_v[i], NN)
    disp[...] = (
        (dot(to_rows, latent.astype(BF16), TN) + dot(to_cot, cot[...], TN))
        .astype(BF16)
        .reshape(disp.shape)
    )
    squeeze[...] = picks((2 * brow, block), 0, brow)
    stretch[...] = picks((block, 2 * brow), 1, brow)
    pl.semaphore_wait(barrier, groups + ring - 1)

    cot_copies = []
    for i in range(1, ring):
        copy = pltpu.make_async_remote_copy(
            src_ref=cot,
            dst_ref=cot_all.at[me_x],
            send_sem=cot_send.at[i - 1],
            recv_sem=cot_recv.at[i - 1],
            device_id={"tensor": (me_x + i) % ring},
            device_id_type=MESH,
        )
        cot_copies.append(copy)

    def to_batch(p, sign, send):
        lines_there = [
            (me_line + (by if sign > 0 else lines - by)) % lines for by in (p, lines - 1 - p)
        ]

        def four(by, skip):
            for odd in (0, 1):
                place = by + odd * (span - 1 - 2 * by)
                place_there = (me_place + (place if sign > 0 else span - place)) % span
                for line_odd in (0, 1):
                    if not (skip and odd == 0 and line_odd == 0):
                        q = 4 * by + 2 * odd + line_odd
                        send(p * batch + q, lines_there[line_odd] * span + place_there)

        if p == 0:
            four(0, True)
        if p > 0 or span > 2:
            pl.loop(1 if p == 0 else 0, span // 2)(lambda by: four(by, False))

    def dispatch(p):
        def send(index, there):
            pltpu.make_async_remote_copy(
                src_ref=disp.at[there],
                dst_ref=land.at[index],
                send_sem=a2a_send.at[0],
                recv_sem=land_sem.at[p],
                device_id={"expert": there},
                device_id_type=MESH,
            ).start()

        to_batch(p, 1, send)

    order = [*range(1, batches), 0]
    own = pltpu.make_async_copy(disp.at[me_e], land.at[0], own_sem.at[0])
    own.start()
    for p in order[:2]:
        dispatch(p)
    for copy in cot_copies:
        copy.start()

    def dispatch_wide():
        for copy in cot_copies:
            copy.wait_recv()
        for s in range(half):
            part = dot(near_map[0], cot_all[s], TN) + dot(near_map[1], cot_all[half + s], TN)
            part = part.astype(BF16).reshape(batch, 2 * PAD, wide)
            disp_wide[:, :, s * wide : (s + 1) * wide] = part

        def send(index, there):
            pltpu.make_async_remote_copy(
                src_ref=disp_wide.at[index],
                dst_ref=land_wide.at[index],
                send_sem=wide_sem.at[0],
                recv_sem=wide_sem.at[1],
                device_id={"expert": there},
                device_id_type=MESH,
            ).start()

        to_batch(0, 1, send)
        pltpu.make_async_copy(disp_wide.at[0], land_wide.at[0], own_sem.at[2]).start()

    def enter_wide():
        pltpu.make_async_copy(disp_wide.at[0], land_wide.at[0], own_sem.at[2]).wait()
        many(land_wide, 1, batch - 1, wide_sem.at[0], wide_sem.at[1]).wait_recv()
        total = jnp.zeros((brow, hid), F32)
        for s in range(half):
            part = land_wide[:, :, s * wide : (s + 1) * wide].reshape(block, wide)
            packed = dot(squeeze[...], part, NN).astype(BF16)
            ag[0, s, BACK] = packed[:brow]
            ag[0, half + s, BACK] = packed[brow:]
            total = total + dot(packed[:brow], wo[s], NT) + dot(packed[brow:], wo[half + s], NT)
        acc_a[0] = total

    def many(buffer, first, count, send_sem, recv_sem):
        part = buffer.at[pl.ds(first, count)]
        return pltpu.make_async_remote_copy(
            src_ref=part,
            dst_ref=part,
            send_sem=send_sem,
            recv_sem=recv_sem,
            device_id={"expert": (me_e + 1) % groups},
            device_id_type=MESH,
        )

    def passed(buffer, index, sems, way, p, step):
        send, recv = sems
        return pltpu.make_async_remote_copy(
            src_ref=buffer[0].at[index],
            dst_ref=buffer[1].at[index],
            send_sem=send.at[way, p, step - 1],
            recv_sem=recv.at[way, p, step - 1],
            device_id={"tensor": toward[way]},
            device_id_type=MESH,
        )

    halves = ((R, OUT), (L_, BACK))
    ag_copies, rs_copies, ret_copies, dp_copies, stores = {}, {}, [], [], []

    def gather(p, step):
        for way, part in halves:
            owner = (me_x + (ring - step + 1 if way == R else step - 1)) % ring
            index = (p, owner, part) if step == half else (p, owner)
            if p == 0:
                if step == half and part == BACK:
                    continue
                index = (p, owner, OUT)
            copy = passed((ag, ag), index, (ag_send, ag_recv), way, p, step)
            copy.start()
            ag_copies[way, p, step] = copy

    def absorb(p, owner, first=False):
        h = dot(ag[p, owner, OUT], wgu[owner], NN)
        if first:
            acc_h[p] = h
        else:
            acc_h[p] += h
        if p > 0:
            a = dot(ag[p, owner, BACK], wo[owner], NT)
            if first:
                acc_a[p] = a
            else:
                acc_a[p] += a

    def enter(p):
        if p == 0:
            own.wait()
            many(land, 1, batch - 1, a2a_send.at[0], land_sem.at[0]).wait_recv()
        else:
            many(land, 0, batch, a2a_send.at[0], land_sem.at[p]).wait_recv()
        packed = dot(squeeze[...], land[p * batch : (p + 1) * batch].reshape(block, wide), NN)
        packed = packed.astype(BF16)
        ag[p, me_x, OUT] = packed[:brow]
        if p > 0:
            ag[p, me_x, BACK] = packed[brow:]
        gather(p, 1)
        if p in order[:-2]:
            dispatch(order[order.index(p) + 2])
        if p == order[0]:
            for copy in weight_copies:
                copy.wait()
        absorb(p, me_x, first=True)

    def forward(p, step):
        for way in (R, L_):
            if (way, p, step) in ag_copies:
                ag_copies[way, p, step].wait_recv()
        if step < half:
            gather(p, step + 1)
            absorb(p, (me_x + ring - step) % ring)
        absorb(p, (me_x + step) % ring)

    def activate(p):
        pre_gate, pre_up, act_grad = acc_h[p, :, :hid], acc_h[p, :, hid:], acc_a[p]
        sig = jax.nn.sigmoid(pre_gate)
        silu = pre_gate * sig
        act[p] = (silu * pre_up).astype(BF16)
        gug[p, :, :hid] = (act_grad * pre_up * sig * (1.0 + pre_gate * (1.0 - sig))).astype(BF16)
        gug[p, :, hid:] = (act_grad * silu).astype(BF16)

    def contribution(p, part, owner):
        if part == OUT:
            return dot(act[p], wo[owner], NN)
        return dot(gug[p], wgu[owner], NT)

    def push(p, step):
        ahead = half + 1 - step
        for way, part in halves:
            owner = (me_x + (ahead if way == R else ring - ahead)) % ring
            if step == 1:
                rs_send[way, p, 0, part] = contribution(p, part, owner).astype(BF16)
                index = (way, p, 0, part)
            else:
                values = [contribution(p, both, owner) for both in (OUT, BACK)]
                rs_copies[way, p, step - 1].wait_recv()
                for both in (OUT, BACK):
                    if step > 2 or both == part:
                        values[both] = values[both] + rs_recv[way, p, step - 2, both].astype(F32)
                    rs_send[way, p, step - 1, both] = values[both].astype(BF16)
                index = (way, p, step - 1)
            copy = passed((rs_send, rs_recv), index, (rs_ssem, rs_rsem), way, p, step)
            copy.start()
            rs_copies[way, p, step] = copy

    def leave(p):
        values = [contribution(p, both, me_x) for both in (OUT, BACK)]
        for way, part in halves:
            rs_copies[way, p, half].wait_recv()
            for both in (OUT, BACK):
                if half > 1 or both == part:
                    values[both] = values[both] + rs_recv[way, p, half - 1, both].astype(F32)
        for both in (OUT, BACK):
            fin[p, pl.ds(both * brow, brow), :] = values[both].astype(BF16)
        spread = dot(stretch[...], fin[p], NN).astype(BF16)
        ret[p * batch : (p + 1) * batch] = spread.reshape(batch, 2 * PAD, wide)

        def send(index, there):
            pltpu.make_async_remote_copy(
                src_ref=ret.at[index],
                dst_ref=home.at[me_e],
                send_sem=a2a_send.at[1],
                recv_sem=home_sem.at[0],
                device_id={"expert": there},
                device_id_type=MESH,
            ).start()

        to_batch(p, -1, send)

        if p == 0:
            ret_copies.append(pltpu.make_async_copy(ret.at[0], home.at[me_e], own_sem.at[1]))
            ret_copies[0].start()

    def grads_of(owner):
        lat = ag[:, owner, OUT].reshape(rows, wide)
        cots = ag[:, owner, BACK].reshape(rows, wide)
        return dot(lat, gug[...].reshape(rows, 2 * hid), TN), dot(act_t[...], cots, NN)

    def for_peer(i):
        if i == 0:
            act_t[...] = act[...].reshape(rows, hid).T
        gu, o = grads_of(peer_d * half + i)
        dp_gu_send[i] = gu.astype(BF16)
        dp_o_send[i] = o.astype(BF16)
        for j, (src, dst) in enumerate(((dp_gu_send, dp_gu_recv), (dp_o_send, dp_o_recv))):
            copy = pltpu.make_async_remote_copy(
                src_ref=src.at[i],
                dst_ref=dst.at[i],
                send_sem=dp_ssem.at[j, i],
                recv_sem=dp_rsem.at[j, i],
                device_id={"dp": peer_d},
                device_id_type=MESH,
            )
            copy.start()
            dp_copies.append(copy)

    def for_self(i):
        gu, o = grads_of(me_d * half + i)
        for copy in dp_copies[2 * i : 2 * i + 2]:
            copy.wait_recv()
        stage_gu[i] = (gu + dp_gu_recv[i].astype(F32)).astype(BF16)
        stage_o[i] = (o + dp_o_recv[i].astype(F32)).astype(BF16)
        for j, (src, dst) in enumerate(
            (
                (stage_gu.at[i, :, pl.ds(0, hid)], grad_gate.at[0, pl.ds(i * wide, wide), :]),
                (stage_gu.at[i, :, pl.ds(hid, hid)], grad_up.at[0, pl.ds(i * wide, wide), :]),
                (stage_o.at[i], grad_out.at[0, :, pl.ds(i * wide, wide)]),
            )
        ):
            copy = pltpu.make_async_copy(src, dst, store_sem.at[j, i])
            copy.start()
            stores.append(copy)

    tasks = [functools.partial(for_peer, i) for i in range(half)]
    tasks += [functools.partial(for_self, i) for i in range(half)]

    for tick in range(2 * half + batches):
        if tick < batches:
            enter(order[tick])
        for place, p in reversed(list(enumerate(order))):
            at = tick - place
            if 1 <= at <= half:
                forward(p, at)
                if at == half:
                    if p == 0:
                        enter_wide()
                    activate(p)
                    push(p, 1)
            elif half < at < 2 * half:
                push(p, at - half + 1)
            elif at == 2 * half:
                leave(p)
            if tick > half + batches - 1 and tasks:
                tasks.pop(0)()
        if tick == 1:
            dispatch_wide()
    for task in tasks:
        task()

    many(disp_wide, 1, batch - 1, wide_sem.at[0], wide_sem.at[1]).wait_send()
    for copy in (*cot_copies, *ag_copies.values(), *rs_copies.values(), *dp_copies):
        copy.wait_send()
    for copy in stores:
        copy.wait()
    many(disp, 0, groups - 1, a2a_send.at[0], land_sem.at[0]).wait_send()

    for copy in ret_copies:
        copy.wait()
    homeward = many(home, 0, groups - 1, a2a_send.at[1], home_sem.at[0])
    homeward.wait_recv()
    back = home[...].reshape(groups * 2 * PAD, wide)
    latent_out[...] = dot(comb[0], back, NN).astype(BF16)
    latent_grad[...] = dot(comb[1], back, NN).astype(BF16)
    homeward.wait_send()


def hand_on(count, *refs):
    given, results, held = refs[:count], refs[count : 2 * count], refs[2 * count : 3 * count]
    sems = refs[-1]
    loads = [pltpu.make_async_copy(given[i], held[i], sems.at[0, i]) for i in range(count)]
    stores = [pltpu.make_async_copy(held[i], results[i], sems.at[1, i]) for i in range(count)]
    for copy in loads:
        copy.start()
    for load, store in zip(loads, stores):
        load.wait()
        store.start()
    for copy in stores:
        copy.wait()


def per_device(tokens, w_latent, w_gate, w_up, w_out, expert_ids, gates, cotangent):
    groups, ring = lax.axis_size("expert"), lax.axis_size("tensor")
    half = ring // 2
    tok, width = tokens.shape
    wide = cotangent.shape[1]
    hid = w_gate.shape[2]
    rows = groups * CAP
    span = 1
    while (2 * span) ** 2 <= groups:
        span = 2 * span
    batch, batches = 2 * span, groups // (2 * span)
    brow, block = batch * CAP, batch * 2 * PAD
    lat_steps = 8
    depth = width // lat_steps
    dma = pltpu.SemaphoreType.DMA
    vmem = pl.BlockSpec(memory_space=pltpu.VMEM)
    hbm = pl.BlockSpec(memory_space=pl.ANY)
    flops = 2 * tok * width * wide + 18 * rows * ring * wide * hid
    outs = pl.pallas_call(
        functools.partial(kernel, (groups, span, ring, lat_steps)),
        out_shape=(
            jax.ShapeDtypeStruct((tok, wide), BF16),
            jax.ShapeDtypeStruct((tok, wide), BF16),
            jax.ShapeDtypeStruct((1, half * wide, hid), BF16),
            jax.ShapeDtypeStruct((1, half * wide, hid), BF16),
            jax.ShapeDtypeStruct((1, hid, half * wide), BF16),
        ),
        in_specs=[hbm] * 5 + [vmem] * 3,
        out_specs=(vmem, vmem, hbm, hbm, hbm),
        scratch_shapes=[
            pltpu.VMEM((lat_steps, tok, depth), BF16),
            pltpu.VMEM((lat_steps, depth, wide), BF16),
            pltpu.VMEM((ring, wide, 2 * hid), BF16),
            pltpu.VMEM((ring, hid, wide), BF16),
            pltpu.VMEM((2, tok, groups * 2 * PAD), BF16),
            pltpu.VMEM((groups, 2 * PAD, wide), BF16),
            pltpu.VMEM((groups, 2 * PAD, wide), BF16),
            pltpu.VMEM((batches, ring, 2, brow, wide), BF16),
            pltpu.VMEM((batches, brow, 2 * hid), F32),
            pltpu.VMEM((batches, brow, hid), F32),
            pltpu.VMEM((batches, brow, hid), BF16),
            pltpu.VMEM((hid, rows), BF16),
            pltpu.VMEM((batches, brow, 2 * hid), BF16),
            pltpu.VMEM((2, batches, half, 2, brow, wide), BF16),
            pltpu.VMEM((2, batches, half, 2, brow, wide), BF16),
            pltpu.VMEM((batches, 2 * brow, wide), BF16),
            pltpu.VMEM((groups, 2 * PAD, wide), BF16),
            pltpu.VMEM((groups, 2 * PAD, wide), BF16),
            pltpu.VMEM((2 * brow, block), BF16),
            pltpu.VMEM((block, 2 * brow), BF16),
            pltpu.VMEM((2, tok, block), BF16),
            pltpu.VMEM((ring, tok, wide), BF16),
            pltpu.VMEM((batch, 2 * PAD, half * wide), BF16),
            pltpu.VMEM((batch, 2 * PAD, half * wide), BF16),
            pltpu.VMEM((half, wide, 2 * hid), BF16),
            pltpu.VMEM((half, wide, 2 * hid), BF16),
            pltpu.VMEM((half, hid, wide), BF16),
            pltpu.VMEM((half, hid, wide), BF16),
            pltpu.VMEM((half, wide, 2 * hid), BF16),
            pltpu.VMEM((half, hid, wide), BF16),
            dma((2 + ring,)),
            dma((2, lat_steps)),
            dma((3,)),
            dma((2,)),
            dma((batches,)),
            dma((1,)),
            dma((2,)),
            dma((ring - 1,)),
            dma((ring - 1,)),
            dma((2, batches, half)),
            dma((2, batches, half)),
            dma((2, batches, half)),
            dma((2, batches, half)),
            dma((2, half)),
            dma((2, half)),
            dma((3, half)),
        ],
        compiler_params=pltpu.CompilerParams(
            collective_id=0, has_side_effects=True, vmem_limit_bytes=56 * 1024 * 1024
        ),
        cost_estimate=pl.CostEstimate(
            flops=flops, bytes_accessed=10 * 1024 * 1024, transcendentals=rows * hid
        ),
    )(
        tokens,
        w_latent,
        w_gate.reshape(ring, wide, hid),
        w_up.reshape(ring, wide, hid),
        w_out,
        expert_ids.T,
        gates.T,
        cotangent,
    )
    return pl.pallas_call(
        functools.partial(hand_on, len(outs)),
        out_shape=tuple(jax.ShapeDtypeStruct(out.shape, out.dtype) for out in outs),
        in_specs=[hbm] * len(outs),
        out_specs=(hbm,) * len(outs),
        scratch_shapes=[pltpu.VMEM(out.shape, out.dtype) for out in outs] + [dma((2, len(outs)))],
        compiler_params=pltpu.CompilerParams(vmem_limit_bytes=60 * 1024 * 1024),
    )(*outs)


def solution(mesh):
    in_specs = (
        P(("dp", "expert"), None),
        P(None, "tensor"),
        P("expert", None, "tensor"),
        P("expert", None, "tensor"),
        P("expert", "tensor", None),
        P(("dp", "expert"), None),
        P(("dp", "expert"), None),
        P(("dp", "expert"), "tensor"),
    )
    out_specs = (
        P(("dp", "expert"), "tensor"),
        P(("dp", "expert"), "tensor"),
        P("expert", "dp", "tensor"),
        P("expert", "dp", "tensor"),
        P("expert", "tensor", "dp"),
    )
    return jax.shard_map(
        per_device, mesh=mesh, in_specs=in_specs, out_specs=out_specs, check_vma=False
    )
```
